512 devices in a mesh: inner: 8 (over y_lo, x), outer: 64 (over y_hi, z, core).
Axes of the slice: x: 4, y: 4 (y_hi: 2, y_lo: 2; y = y_hi * 2 + y_lo), z: 16, core: 2. Of those that a mesh axis runs over, the one named last changes fastest.
Arguments:
- tokens: bfloat16 [65536, 4096], P(('inner', 'outer')), may hold values from -24 to 24
- grad_out: bfloat16 [65536, 4096], P(('inner', 'outer')), may hold values from -24 to 24
- quant_weights: bfloat16 [3, 32, 128, 512], P(None, 'inner'), may hold values from -0.09375 to 0.09375
- block_scales: float32 [3, 32, 512], P(None, 'inner'), may hold values from 0.5 to 2
Outputs:
- input_grad: bfloat16 [65536, 4096], P(('inner', 'outer'))
- weight_grads: float32 [3, 4096, 512], P(None, ('inner', 'outer'))
The draws below stay inside these ranges and needn't reach their ends.
All inputs are finite; a program needn't handle non-finite values.
Results may differ from the reference program's by a relative error of at most 0.028.
Values may be sent and summed in bfloat16 or wider, within the bound.
A program may use at most 128 MiB of HBM per device.

```python
import math
import jax
import jax.numpy as jnp
from jax import lax

D = 4096
HID = 512
BLOCK = 128
TOK_DEV = 128
TOKENS = 65536


def spiked(drawn, rng, source, target, parts, factor):
    def block_of(position):
        return (jnp.arange(drawn.shape[position]) // (drawn.shape[position] // parts)).reshape((-1,) + (1,) * (drawn.ndim - 1 - position))

    first = jax.random.permutation(rng, parts)[block_of(target)]
    second = (block_of(target) + parts // 2) % parts
    return jnp.where((block_of(source) == first) | (block_of(source) == second), factor * drawn, drawn)


def block_scale(key, extent, shards, least, top_value):
    factor_of = 1.0
    for position, shards_of in shards:
        heights = jax.random.uniform(jax.random.fold_in(jax.random.fold_in(key, 6), position), (shards_of,), jnp.float32, least / len(shards), top_value / len(shards))
        factor_of = factor_of * jnp.repeat(jnp.exp(heights), extent[position] // shards_of).reshape((-1,) + (1,) * (len(extent) - 1 - position))
    return factor_of


def gaussian(rng, dims, width, bound, shards=(), dtype=jnp.bfloat16):
    array = jax.random.normal(rng, dims, jnp.float32) * width
    if len(shards) > 0:
        array = block_scale(rng, dims, shards, -0.22, 0.18) * array
    return jnp.clip(array, min=-bound, max=bound).astype(dtype)


def heavy_noise(own_key, dims, spread, most, split, heavy, dtype=jnp.bfloat16):
    result = spread * jax.random.normal(own_key, dims, jnp.float32)
    if split:
        result = result * block_scale(own_key, dims, split, -0.22, 0.18)
    return jnp.clip(spiked(result, jax.random.fold_in(own_key, 3), *heavy), -most, most).astype(dtype)


def setup_inputs(seed: int = 0) -> dict:
    key_of = jax.random.split(jax.random.key(seed), 5)
    return {
        "tokens": heavy_noise(key_of[0], (TOKENS, D), 1.0, 24.0, ((0, 512),), (0, 1, 512, 6.0)),
        "grad_out": heavy_noise(key_of[1], (TOKENS, D), 1.0, 24.0, ((0, 512),), (0, 1, 512, 6.0)),
        "quant_weights": gaussian(key_of[2], (3, D // BLOCK, BLOCK, HID), D ** -0.5, 0.09375, ((1, 8),)),
        "block_scales": jnp.clip(jnp.exp(math.log(2.0) - 1.3862944 * jax.random.uniform(key_of[3], (3, D // BLOCK, HID), jnp.float32) ** block_scale(key_of[3], (3, D // BLOCK, HID), ((1, 8),), -0.2, 0.2)), 0.5, 2.0),
    }


def dequantize(quant_weights, block_scales):
    values = quant_weights.astype(jnp.float32) * block_scales[:, :, None, :]
    return values.astype(jnp.bfloat16).reshape(3, D, HID)

def reference(tokens, grad_out, quant_weights, block_scales):
    weights = dequantize(quant_weights, block_scales)
    gate_pre = jnp.dot(tokens, weights[0], preferred_element_type=jnp.float32)
    up_pre = jnp.dot(tokens, weights[1], preferred_element_type=jnp.float32)
    d_hidden = jnp.dot(grad_out, weights[2], preferred_element_type=jnp.float32)
    sigmoid_gate = jax.nn.sigmoid(gate_pre)
    hidden = (gate_pre * sigmoid_gate * up_pre).astype(jnp.bfloat16)
    grad_up = (d_hidden * gate_pre * sigmoid_gate).astype(jnp.bfloat16)
    grad_gate = (d_hidden * up_pre * sigmoid_gate * (1.0 + gate_pre * (1.0 - sigmoid_gate))).astype(jnp.bfloat16)
    input_grad = jnp.dot(grad_gate, weights[0].T, preferred_element_type=jnp.float32)
    input_grad = (input_grad + jnp.dot(grad_up, weights[1].T, preferred_element_type=jnp.float32)).astype(jnp.bfloat16)
    device_count = TOKENS // TOK_DEV
    tok_blocks = tokens.reshape(device_count, TOK_DEV, D)
    out_blocks = grad_out.reshape(device_count, TOK_DEV, D)
    gate_blocks = grad_gate.reshape(device_count, TOK_DEV, HID)
    up_blocks = grad_up.reshape(device_count, TOK_DEV, HID)
    hidden_blocks = hidden.reshape(device_count, TOK_DEV, HID)

    def accumulate(running, items):
        tok_rows, out_rows, gate_rows, up_rows, hidden_rows = items
        first = jnp.dot(tok_rows.T, gate_rows, preferred_element_type=jnp.float32).astype(jnp.bfloat16)
        second = jnp.dot(tok_rows.T, up_rows, preferred_element_type=jnp.float32).astype(jnp.bfloat16)
        third = jnp.dot(out_rows.T, hidden_rows, preferred_element_type=jnp.float32).astype(jnp.bfloat16)
        stacked = jnp.stack([first, second, third]).astype(jnp.float32)
        return (running + stacked, None)
    starting = jnp.zeros((3, D, HID), jnp.float32)
    total, unused = lax.scan(accumulate, starting, (tok_blocks, out_blocks, gate_blocks, up_blocks, hidden_blocks))
    weight_grads = total * (1.0 / jnp.sqrt(jnp.float32(TOKENS)))
    return (input_grad, weight_grads)
```

```python
import functools

import jax
import jax.numpy as jnp
from jax import lax
from jax.experimental import pallas as pl
from jax.experimental.pallas import tpu as pltpu
from jax.sharding import PartitionSpec as P

MESH = pl.DeviceIdType.MESH
BF16, F32 = jnp.bfloat16, jnp.float32
NX, NY, NZ = 4, 4, 16
TOK = 128
HALF = 2048
HK = 256
Q = 256
NT = (((1,), (1,)), ((), ()))


def aligned(index, size):
    return pl.ds(pl.multiple_of(index * size, size), size)


def dot(a, b):
    return jnp.dot(a, b, preferred_element_type=F32)


def kernel(
    tok_hbm, out_hbm, quant_hbm, scales,
    ig_hbm, wg_ref,
    xt, xg, quant, w, pacc, psend, precv, gn, gt, dws, own, relay, near, far,
    ysend, yrecv, zsend, zrecv, fsend, frecv, igk, igs, igr, igo,
    local_sem, xs_sem, xr_sem, ws_sem, wr_sem, ps_sem, pr_sem, rs_sem, rr_sem,
    ys_sem, yr_sem, zs_sem, zr_sem, is_sem, ir_sem, fs_sem, fr_sem,
):
    inner, outer = lax.axis_index("inner"), lax.axis_index("outer")
    x, y_lo = lax.rem(inner, NX), lax.div(inner, NX)
    core, z = lax.rem(outer, 2), lax.rem(lax.div(outer, 2), NZ)
    y_hi = lax.div(outer, 2 * NZ)
    y = 2 * y_hi + y_lo
    other = 1 - core

    def device(dx=0, dy=0, dz=0, at=core):
        to_x, to_y, to_z = (
            lax.rem(x + dx + NX, NX),
            lax.rem(y + dy + NY, NY),
            lax.rem(z + dz + NZ, NZ),
        )
        return (
            lax.rem(to_y, 2) * NX + to_x,
            (lax.div(to_y, 2) * NZ + to_z) * 2 + at,
        )

    sent = []

    def send(src, dst, s_sem, r_sem, to):
        copy = pltpu.make_async_remote_copy(
            src_ref=src, dst_ref=dst, send_sem=s_sem, recv_sem=r_sem, device_id=to, device_id_type=MESH
        )
        copy.start()
        sent.append((src, s_sem))

    def wait(ref, sem):
        pltpu.make_async_copy(ref, ref, sem).wait()

    side = 1 - 2 * core
    mine, theirs = aligned(y_lo, HALF), aligned(1 - y_lo, HALF)
    hidden_half = aligned(core, HK)

    own_rows = aligned(3 * core, TOK)
    pltpu.make_async_copy(quant_hbm.at[:, :, :, hidden_half], quant, local_sem.at[0]).start()
    pltpu.make_async_copy(tok_hbm.at[:, mine], xt.at[own_rows, :], local_sem.at[1]).start()
    pltpu.make_async_copy(out_hbm.at[:, mine], xg.at[own_rows, :], local_sem.at[2]).start()

    barrier = pltpu.get_barrier_semaphore()
    partners = [
        device(at=other), device(dx=1), device(dx=-1), device(dy=1), device(dy=-1), device(dy=2),
        device(dy=side, at=other),
    ]
    for to in partners:
        pl.semaphore_signal(barrier, inc=1, device_id=to, device_id_type=MESH)

    def greet(j, carry):
        pl.semaphore_signal(barrier, inc=1, device_id=device(dz=j), device_id_type=MESH)
        return carry

    lax.fori_loop(1, NZ, greet, 0)
    pl.semaphore_wait(barrier, len(partners) + NZ - 1)

    def send_tokens(a, src, dst):
        away = aligned(2 - core, TOK)
        for part in range(2):
            rows = pl.ds(part * 64, 64)
            to_rows = pl.ds(pl.multiple_of((2 - core) * TOK + part * 64, 64), 64)
            send(
                src.at[rows, theirs], dst.at[to_rows, :], xs_sem.at[a, part], xr_sem.at[a, core],
                device(dy=side, at=part),
            )
        send(src.at[:, mine], dst.at[own_rows, :], xs_sem.at[a, 2], xr_sem.at[a, 2], device(at=other))

    def dequantise(m):
        for b in range(4):
            scale = scales[m, pl.ds(b, 1), hidden_half]
            w[m, x, b * 128 : (b + 1) * 128, :] = (quant[m, b].astype(F32) * scale).astype(BF16)

    def send_weights(m):
        block = w.at[m, x]
        send(block, block, ws_sem.at[m, 0], wr_sem.at[m, 0], device(dx=1))
        send(block, block, ws_sem.at[m, 1], wr_sem.at[m, 1], device(dx=-1))

    before, after = lax.rem(x + 3, NX), lax.rem(x + 1, NX)
    across = lax.rem(x + 2, NX)

    def relay_weights(m):
        wait(w.at[m, before], wr_sem.at[m, 0])
        block = w.at[m, before, pl.ds(0, Q), :]
        send(block, block, ws_sem.at[m, 2], wr_sem.at[m, 2], device(dx=1))
        wait(w.at[m, after], wr_sem.at[m, 1])
        block = w.at[m, after, pl.ds(Q, Q), :]
        send(block, block, ws_sem.at[m, 3], wr_sem.at[m, 3], device(dx=-1))

    wait(quant, local_sem.at[0])
    send_tokens(0, tok_hbm, xt)
    dequantise(0)
    send_weights(0)
    dequantise(1)
    send_weights(1)
    dequantise(2)
    send_tokens(1, out_hbm, xg)

    def pass_tokens(a, dst):
        for i, block in enumerate((2, 1)):
            rows = pl.ds(pl.multiple_of(block * TOK + core * 64, 64), 64)
            wait(dst.at[rows, :], xr_sem.at[a, i])
            send(dst.at[rows, :], dst.at[rows, :], xs_sem.at[a, 3 + i], xr_sem.at[a, 3 + i], device(at=other))

    def wait_tokens(a, dst):
        wait(dst.at[own_rows, :], local_sem.at[1 + a])
        wait(dst.at[aligned(3 - 3 * core, TOK), :], xr_sem.at[a, 2])
        for i, block in enumerate((2, 1)):
            rows = pl.ds(pl.multiple_of(block * TOK + other * 64, 64), 64)
            wait(dst.at[rows, :], xr_sem.at[a, 3 + i])

    def term(m, block):
        rows = (xg if m == 2 else xt)[:, aligned(block, 512)]
        return dot(rows, w[m, block])

    def first_terms(m):
        pacc[m] = term(m, x) + term(m, before) + term(m, after)

    def last_term(m):
        wait(w.at[m, across, pl.ds(0, Q), :], wr_sem.at[m, 2])
        wait(w.at[m, across, pl.ds(Q, Q), :], wr_sem.at[m, 3])
        total = pacc[m] + term(m, across)
        pacc[m] = total
        psend[m] = total.astype(BF16)
        send(psend.at[m, pl.ds(0, 256)], precv.at[m, pl.ds(256, 256)], ps_sem.at[m, 0], pr_sem.at[m, 0], device(dy=1))
        send(psend.at[m, pl.ds(256, 256)], precv.at[m, pl.ds(0, 256)], ps_sem.at[m, 1], pr_sem.at[m, 1], device(dy=-1))

    relay_weights(0)
    send_weights(2)
    pass_tokens(0, xt)
    wait_tokens(0, xt)
    first_terms(0)
    relay_weights(1)
    first_terms(1)
    pass_tokens(1, xg)
    last_term(0)
    wait_tokens(1, xg)
    relay_weights(2)
    first_terms(2)
    last_term(1)
    last_term(2)

    for m in range(3):
        wait(precv.at[m, pl.ds(256, 256)], pr_sem.at[m, 0])
        wait(precv.at[m, pl.ds(0, 256)], pr_sem.at[m, 1])

    def elementwise(b, carry):
        rows = aligned(b, 128)
        gate, up, d_hidden = (pacc[m, rows, :] + precv[m, rows, :].astype(F32) for m in range(3))
        s = jax.nn.sigmoid(gate)
        hidden = (gate * s * up).astype(BF16)
        grad_up = (d_hidden * gate * s).astype(BF16)
        grad_gate = (d_hidden * up * s * (1.0 + gate * (1.0 - s))).astype(BF16)
        gn[0, rows, :] = grad_gate
        gn[1, rows, :] = grad_up
        gt[0, :, rows] = grad_gate.T
        gt[1, :, rows] = grad_up.T
        gt[2, :, rows] = hidden.T
        return carry

    lax.fori_loop(0, 4, elementwise, 0)

    def product(m, block, half):
        columns = aligned(block * 2 + half, Q)
        return dot(gt[m], (xg if m == 2 else xt)[:, columns])

    def send_across(m):
        for half, step in ((0, 1), (1, -1)):
            dws[m, half] = product(m, across, half).astype(BF16)
            send(dws.at[m, half], relay.at[m, half], rs_sem.at[m, half], rr_sem.at[m, half], device(dx=step))

    def send_near(m):
        for half, step, block in ((0, -1, before), (1, 1, after)):
            dws[m, 2 + half] = product(m, block, half).astype(BF16)
            send(
                dws.at[m, 2 + half], near.at[m, half], rs_sem.at[m, 2 + half], rr_sem.at[m, 2 + half],
                device(dx=step),
            )

    def send_far(m):
        for half, step, block in ((0, 1, after), (1, -1, before)):
            value = product(m, block, half)
            wait(relay.at[m, half], rr_sem.at[m, half])
            dws[m, 4 + half] = (value + relay[m, half].astype(F32)).astype(BF16)
            send(
                dws.at[m, 4 + half], far.at[m, half], rs_sem.at[m, 4 + half], rr_sem.at[m, 4 + half],
                device(dx=step),
            )

    def keep(m):
        for half in range(2):
            own[m, half] = product(m, x, half)

    def across_y(m):
        for half in range(2):
            wait(near.at[m, half], rr_sem.at[m, 2 + half])
            wait(far.at[m, half], rr_sem.at[m, 4 + half])
        gone = 1 - y_hi
        ysend[m] = (own[m, gone] + near[m, gone].astype(F32) + far[m, gone].astype(F32)).astype(BF16)
        send(ysend.at[m], yrecv.at[m], ys_sem.at[m], yr_sem.at[m], device(dy=2))
        own[m, y_hi] = own[m, y_hi] + near[m, y_hi].astype(F32) + far[m, y_hi].astype(F32)

    def across_z(m):
        wait(yrecv.at[m], yr_sem.at[m])
        total = own[m, y_hi] + yrecv[m].astype(F32)
        zsend[m] = total.T.astype(BF16).reshape(NZ, 16, HK)

        def post(j, carry):
            to_z = lax.rem(z + j, NZ)
            pltpu.make_async_remote_copy(
                src_ref=zsend.at[m, to_z], dst_ref=zrecv.at[m, j - 1], send_sem=zs_sem.at[m],
                recv_sem=zr_sem.at[m], device_id=device(dz=j), device_id_type=MESH,
            ).start()
            return carry

        lax.fori_loop(1, NZ, post, 0)

    def input_grad(b, carry):
        columns = aligned(b, Q)
        block, half = lax.div(b, 2), lax.rem(b, 2)
        rows = aligned(half, Q)
        total = lax.dot_general(gn[0], w[0, block, rows, :], NT, preferred_element_type=F32)
        total += lax.dot_general(gn[1], w[1, block, rows, :], NT, preferred_element_type=F32)

        @pl.when(core == 0)
        def _():
            igk[0, :, columns] = total[0:128]
            igk[1, :, columns] = total[256:384]
            igs[0, :, columns] = total[384:512].astype(BF16)
            igs[1, :, columns] = total[128:256].astype(BF16)

        @pl.when(core == 1)
        def _():
            igk[0, :, columns] = total[384:512]
            igk[1, :, columns] = total[128:256]
            igs[0, :, columns] = total[0:128].astype(BF16)
            igs[1, :, columns] = total[256:384].astype(BF16)

        return carry

    send_across(0)
    send_near(0)
    send_across(1)
    send_far(0)
    send_near(1)
    send_across(2)
    keep(0)
    send_far(1)
    send_near(2)
    keep(1)
    send_far(2)
    keep(2)
    lax.fori_loop(0, 8, input_grad, 0)
    send(igs, igr, is_sem.at[0], ir_sem.at[0], device(at=other))
    across_y(0)
    wait(igr, ir_sem.at[0])
    for slot in range(2):
        igo[slot] = (igk[slot] + igr[slot].astype(F32)).astype(BF16)
    done = pltpu.make_async_copy(igo.at[0], ig_hbm.at[:, mine], local_sem.at[3])
    done.start()
    send(igo.at[1], ig_hbm.at[:, mine], is_sem.at[1], ir_sem.at[1], device(dy=-side))
    across_z(0)
    across_y(1)
    across_z(1)
    across_y(2)
    across_z(2)

    scale = 1.0 / 256.0
    finals = []
    for m in range(3):
        wait(zrecv.at[m], zr_sem.at[m])
        total = zsend[m, z].astype(F32)
        for j in range(NZ - 1):
            total = total + zrecv[m, j].astype(F32)
        finals.append(total * scale)

    @pl.when(core == 0)
    def _():
        for m in range(3):
            wg_ref[m, :, 0:HK] = finals[m][0:8]
            fsend[m] = finals[m][8:16]

    @pl.when(core == 1)
    def _():
        for m in range(3):
            wg_ref[m, :, HK : 2 * HK] = finals[m][8:16]
            fsend[m] = finals[m][0:8]

    send(fsend, frecv, fs_sem, fr_sem, device(at=other))
    wait(frecv, fr_sem)

    @pl.when(core == 0)
    def _():
        wg_ref[:, :, HK : 2 * HK] = frecv[...]

    @pl.when(core == 1)
    def _():
        wg_ref[:, :, 0:HK] = frecv[...]

    done.wait()
    wait(ig_hbm.at[:, theirs], ir_sem.at[1])
    for m in range(3):
        wait(zrecv.at[m], zs_sem.at[m])
    for src, sem in sent:
        wait(src, sem)


def local(tokens, grad_out, quant_weights, block_scales):
    any_space = pl.BlockSpec(memory_space=pl.ANY)
    vmem = pl.BlockSpec(memory_space=pltpu.VMEM)
    dma = pltpu.SemaphoreType.DMA
    return pl.pallas_call(
        kernel,
        out_shape=(
            jax.ShapeDtypeStruct((TOK, 2 * HALF), BF16),
            jax.ShapeDtypeStruct((3, 8, 2 * HK), F32),
        ),
        in_specs=[any_space, any_space, any_space, vmem],
        out_specs=(any_space, vmem),
        scratch_shapes=[
            pltpu.VMEM((4 * TOK, HALF), BF16),
            pltpu.VMEM((4 * TOK, HALF), BF16),
            pltpu.VMEM((3, 4, 128, HK), BF16),
            pltpu.VMEM((3, NX, 512, HK), BF16),
            pltpu.VMEM((3, 4 * TOK, HK), F32),
            pltpu.VMEM((3, 4 * TOK, HK), BF16),
            pltpu.VMEM((3, 4 * TOK, HK), BF16),
            pltpu.VMEM((2, 4 * TOK, HK), BF16),
            pltpu.VMEM((3, HK, 4 * TOK), BF16),
            pltpu.VMEM((3, 6, HK, Q), BF16),
            pltpu.VMEM((3, 2, HK, Q), F32),
            pltpu.VMEM((3, 2, HK, Q), BF16),
            pltpu.VMEM((3, 2, HK, Q), BF16),
            pltpu.VMEM((3, 2, HK, Q), BF16),
            pltpu.VMEM((3, HK, Q), BF16),
            pltpu.VMEM((3, HK, Q), BF16),
            pltpu.VMEM((3, NZ, 16, HK), BF16),
            pltpu.VMEM((3, NZ - 1, 16, HK), BF16),
            pltpu.VMEM((3, 8, HK), F32),
            pltpu.VMEM((3, 8, HK), F32),
            pltpu.VMEM((2, TOK, HALF), F32),
            pltpu.VMEM((2, TOK, HALF), BF16),
            pltpu.VMEM((2, TOK, HALF), BF16),
            pltpu.VMEM((2, TOK, HALF), BF16),
            dma((4,)),
            dma((2, 5)), dma((2, 5)),
            dma((3, 4)), dma((3, 4)),
            dma((3, 2)), dma((3, 2)),
            dma((3, 6)), dma((3, 6)),
            dma((3,)), dma((3,)),
            dma((3,)), dma((3,)),
            dma((2,)), dma((2,)),
            dma, dma,
        ],
        compiler_params=pltpu.CompilerParams(
            collective_id=0, has_side_effects=True, vmem_limit_bytes=56 * 1024 * 1024
        ),
    )(tokens, grad_out, quant_weights, block_scales)


def solution(mesh):
    return jax.shard_map(
        local,
        mesh=mesh,
        in_specs=(
            P(("inner", "outer"), None),
            P(("inner", "outer"), None),
            P(None, "inner", None, None),
            P(None, "inner", None),
        ),
        out_specs=(P(("inner", "outer"), None), P(None, ("inner", "outer"), None)),
        check_vma=False,
    )
```

```python
import jax
import jax.numpy as jnp
from jax import lax
from jax.experimental import pallas as pl
from jax.experimental.pallas import tpu as pltpu
from jax.sharding import PartitionSpec as P

MESH = pl.DeviceIdType.MESH
BF16, F32 = jnp.bfloat16, jnp.float32
NX, NY, NZ = 4, 4, 16
TOK = 128
HALF = 2048
HK = 256
Q = 256
WIDTH = (256, 128, 128)
NT = (((1,), (1,)), ((), ()))


def scratch():
    vmem, dma = pltpu.VMEM, pltpu.SemaphoreType.DMA
    shapes = {
        "xt": vmem((4 * TOK, HALF), BF16),
        "xg": vmem((4 * TOK, HALF), BF16),
        "quant": vmem((3, 4, 128, HK), BF16),
        "w": vmem((3, NX, 512, HK), BF16),
        "pacc": vmem((3, 4 * TOK, HK), F32),
        "psend": vmem((3, 4 * TOK, HK), BF16),
        "precv": vmem((3, 4 * TOK, HK), BF16),
        "gn": vmem((2, 4 * TOK, HK), BF16),
        "gt": vmem((3, HK, 4 * TOK), BF16),
        "pair_keep": vmem((3, NX, 2, HK, 128), F32),
        "pair_send": vmem((3, NX, 2, HK, 128), BF16),
        "pair_recv": vmem((3, NX, 2, HK, 128), BF16),
        "fsend": vmem((3, 8, HK), F32),
        "frecv": vmem((3, 8, HK), F32),
        "igk": vmem((2, TOK, HALF), F32),
        "igs": vmem((2, TOK, HALF), BF16),
        "igr": vmem((2, TOK, HALF), BF16),
        "igo": vmem((2, TOK, HALF), BF16),
        "local_sem": dma((4,)),
        "xs_sem": dma((2, 5)), "xr_sem": dma((2, 5)),
        "ws_sem": dma((3, 10)), "wr_sem": dma((3, 10)),
        "ps_sem": dma((3, 2)), "pr_sem": dma((3, 2)),
        "cs_sem": dma((3, NX, 2)), "cr_sem": dma((3, NX, 2)),
        "rs_sem": dma((3, 6)), "rr_sem": dma((3, 6)),
        "ys_sem": dma((3,)), "yr_sem": dma((3,)),
        "zs_sem": dma((3, NZ)), "zr_sem": dma((3, NZ)),
        "is_sem": dma((2,)), "ir_sem": dma((2,)),
        "fs_sem": dma, "fr_sem": dma,
    }
    for m, width in enumerate(WIDTH):
        shapes |= {
            f"dws{m}": vmem((6, HK, width), BF16),
            f"own{m}": vmem((2, HK, width), F32),
            f"relay{m}": vmem((2, HK, width), BF16),
            f"near{m}": vmem((2, HK, width), BF16),
            f"far{m}": vmem((2, HK, width), BF16),
            f"ysend{m}": vmem((HK, width), BF16),
            f"yrecv{m}": vmem((HK, width), BF16),
            f"zsend{m}": vmem((width // 16, 16, HK), BF16),
            f"zrecv{m}": vmem((width // 16, 16, HK), BF16),
        }
    return shapes


def aligned(index, size):
    return pl.ds(pl.multiple_of(index * size, size), size)


def dot(a, b):
    return jnp.dot(a, b, preferred_element_type=F32)


def kernel(tok_hbm, out_hbm, quant_hbm, scales, ig_hbm, wg_ref, *scratch_refs):
    r = dict(zip(scratch(), scratch_refs, strict=True))
    xt, xg, quant, w, pacc, psend, precv, gn, gt = (
        r[name] for name in ("xt", "xg", "quant", "w", "pacc", "psend", "precv", "gn", "gt")
    )
    pair_keep, pair_send, pair_recv = r["pair_keep"], r["pair_send"], r["pair_recv"]
    fsend, frecv, igk, igs, igr, igo = (r[name] for name in ("fsend", "frecv", "igk", "igs", "igr", "igo"))
    local_sem, xs_sem, xr_sem, ws_sem, wr_sem = (
        r[name] for name in ("local_sem", "xs_sem", "xr_sem", "ws_sem", "wr_sem")
    )
    dws, own, relay, near, far, ysend, yrecv, zsend, zrecv = (
        [r[f"{name}{m}"] for m in range(3)]
        for name in ("dws", "own", "relay", "near", "far", "ysend", "yrecv", "zsend", "zrecv")
    )

    inner, outer = lax.axis_index("inner"), lax.axis_index("outer")
    x, y_lo = lax.rem(inner, NX), lax.div(inner, NX)
    core, z = lax.rem(outer, 2), lax.rem(lax.div(outer, 2), NZ)
    y_hi = lax.div(outer, 2 * NZ)
    y = 2 * y_hi + y_lo
    other = 1 - core
    odd = lax.rem(z, 2)
    before, after, across = (lax.rem(x + step, NX) for step in (3, 1, 2))

    def device(dx=0, dy=0, dz=0, at=core):
        to_x, to_y, to_z = (
            lax.rem(x + dx + NX, NX),
            lax.rem(y + dy + NY, NY),
            lax.rem(z + dz + NZ, NZ),
        )
        return (
            lax.rem(to_y, 2) * NX + to_x,
            (lax.div(to_y, 2) * NZ + to_z) * 2 + at,
        )

    sent = []

    def send(src, dst, s_sem, r_sem, to):
        pltpu.make_async_remote_copy(
            src_ref=src, dst_ref=dst, send_sem=s_sem, recv_sem=r_sem, device_id=to, device_id_type=MESH
        ).start()
        sent.append((src, s_sem))

    def wait(ref, sem):
        pltpu.make_async_copy(ref, ref, sem).wait()

    side = 1 - 2 * core
    mine, theirs = aligned(y_lo, HALF), aligned(1 - y_lo, HALF)
    hidden_half = aligned(core, HK)

    own_rows = aligned(3 * core, TOK)
    pltpu.make_async_copy(quant_hbm.at[:, :, :, hidden_half], quant, local_sem.at[0]).start()
    pltpu.make_async_copy(tok_hbm.at[:, mine], xt.at[own_rows, :], local_sem.at[1]).start()
    pltpu.make_async_copy(out_hbm.at[:, mine], xg.at[own_rows, :], local_sem.at[2]).start()

    barrier = pltpu.get_barrier_semaphore()
    partners = [
        device(at=other), device(dx=1), device(dx=-1), device(dy=1), device(dy=-1), device(dy=2),
        device(dy=side, at=other),
    ]
    for to in partners:
        pl.semaphore_signal(barrier, inc=1, device_id=to, device_id_type=MESH)

    def greet(j, carry):
        pl.semaphore_signal(barrier, inc=1, device_id=device(dz=j), device_id_type=MESH)
        return carry

    lax.fori_loop(1, NZ, greet, 0)

    def dequantise(m):
        for b in range(4):
            scale = scales[m, pl.ds(b, 1), hidden_half]
            w[m, x, b * 128 : (b + 1) * 128, :] = (quant[m, b].astype(F32) * scale).astype(BF16)

    wait(quant, local_sem.at[0])
    dequantise(0)
    pl.semaphore_wait(barrier, len(partners) + NZ - 1)

    def send_tokens(a, src, dst):
        for part in range(2):
            rows = pl.ds(part * 64, 64)
            to_rows = pl.ds(pl.multiple_of((2 - core) * TOK + part * 64, 64), 64)
            send(
                src.at[rows, theirs], dst.at[to_rows, :], xs_sem.at[a, part], xr_sem.at[a, core],
                device(dy=side, at=part),
            )
        send(src.at[:, mine], dst.at[own_rows, :], xs_sem.at[a, 2], xr_sem.at[a, 2], device(at=other))

    def pass_tokens(a, dst):
        for i, block in enumerate((2, 1)):
            rows = pl.ds(pl.multiple_of(block * TOK + core * 64, 64), 64)
            wait(dst.at[rows, :], xr_sem.at[a, i])
            send(dst.at[rows, :], dst.at[rows, :], xs_sem.at[a, 3 + i], xr_sem.at[a, 3 + i], device(at=other))

    def wait_tokens(a, dst):
        wait(dst.at[own_rows, :], local_sem.at[1 + a])
        wait(dst.at[aligned(3 - 3 * core, TOK), :], xr_sem.at[a, 2])
        for i, block in enumerate((2, 1)):
            rows = pl.ds(pl.multiple_of(block * TOK + other * 64, 64), 64)
            wait(dst.at[rows, :], xr_sem.at[a, 3 + i])

    def quarter(m, shard, half, q):
        return w.at[m, shard, pl.ds(pl.multiple_of(half * 256 + q * 128, 128), 128), :]

    def half_of(m, shard):
        return w.at[m, shard, aligned(odd, 256), :]

    def pass_on(m, ref, channel, to):
        send(ref, ref, ws_sem.at[m, channel], wr_sem.at[m, channel], to)

    def send_weights(m):
        pass_on(m, half_of(m, x), 0, device(dx=1))
        pass_on(m, half_of(m, x), 1, device(dx=-1))

    def relay_weights(m):
        for i, (shard, step) in enumerate(((before, 1), (after, -1))):
            wait(half_of(m, shard), wr_sem.at[m, i])
            pass_on(m, quarter(m, shard, odd, i), 2 + i, device(dx=step))
            pass_on(m, quarter(m, shard, odd, 0), 4 + 2 * i, device(dz=1))
            pass_on(m, quarter(m, shard, odd, 1), 5 + 2 * i, device(dz=-1))

    def relay_across(m):
        for q, step in ((0, 1), (1, -1)):
            wait(quarter(m, across, odd, q), wr_sem.at[m, 2 + q])
            pass_on(m, quarter(m, across, odd, q), 8 + q, device(dz=step))

    def term(m, shard, half):
        columns = aligned(shard * 2 + half, 256)
        return dot((xg if m == 2 else xt)[:, columns], w[m, shard, aligned(half, 256), :])

    def first_terms(m):
        pacc[m] = term(m, x, 0) + term(m, x, 1) + term(m, before, odd) + term(m, after, odd)

    def last_terms(m):
        for i, shard in enumerate((before, after, across)):
            for q in range(2):
                wait(quarter(m, shard, 1 - odd, q), wr_sem.at[m, 4 + 2 * i + q])
        total = (
            pacc[m] + term(m, before, 1 - odd) + term(m, after, 1 - odd)
            + term(m, across, 0) + term(m, across, 1)
        )
        pacc[m] = total
        psend[m] = total.astype(BF16)
        low, high = pl.ds(0, 256), pl.ds(256, 256)
        send(psend.at[m, low], precv.at[m, high], r["ps_sem"].at[m, 0], r["pr_sem"].at[m, 0], device(dy=1))
        send(psend.at[m, high], precv.at[m, low], r["ps_sem"].at[m, 1], r["pr_sem"].at[m, 1], device(dy=-1))

    send_weights(0)
    send_tokens(0, tok_hbm, xt)
    dequantise(1)
    send_weights(1)
    send_tokens(1, out_hbm, xg)
    dequantise(2)
    relay_weights(0)
    send_weights(2)
    relay_weights(1)
    relay_across(0)
    pass_tokens(0, xt)
    relay_weights(2)
    relay_across(1)
    wait_tokens(0, xt)
    first_terms(0)
    relay_across(2)
    last_terms(0)
    first_terms(1)
    pass_tokens(1, xg)
    last_terms(1)
    wait_tokens(1, xg)
    first_terms(2)
    last_terms(2)

    for m in range(3):
        wait(precv.at[m, pl.ds(256, 256)], r["pr_sem"].at[m, 0])
        wait(precv.at[m, pl.ds(0, 256)], r["pr_sem"].at[m, 1])

    def elementwise(b, carry):
        rows = aligned(b, 128)
        gate, up, d_hidden = (pacc[m, rows, :] + precv[m, rows, :].astype(F32) for m in range(3))
        s = jax.nn.sigmoid(gate)
        hidden = (gate * s * up).astype(BF16)
        grad_up = (d_hidden * gate * s).astype(BF16)
        grad_gate = (d_hidden * up * s * (1.0 + gate * (1.0 - s))).astype(BF16)
        gn[0, rows, :] = grad_gate
        gn[1, rows, :] = grad_up
        gt[0, :, rows] = grad_gate.T
        gt[1, :, rows] = grad_up.T
        gt[2, :, rows] = hidden.T
        return carry

    lax.fori_loop(0, 4, elementwise, 0)

    def product(m, block, half):
        return dot(gt[m], (xg if m == 2 else xt)[:, aligned(block * 2 + half, Q)])

    def pair(m, block):
        for half in range(2):
            value = product(m, block, half)
            low, high = value[:, :128], value[:, 128:]
            pair_keep[m, block, half] = jnp.where(odd == 0, low, high)
            pair_send[m, block, half] = jnp.where(odd == 0, high, low).astype(BF16)
        for part, step in ((0, 1), (1, -1)):
            rows = pl.ds(part * 128, 128)
            send(
                pair_send.at[m, block, :, rows, :], pair_recv.at[m, block, :, rows, :],
                r["cs_sem"].at[m, block, part], r["cr_sem"].at[m, block, part], device(dz=step),
            )

    def wait_pair(m, block):
        if WIDTH[m] == 128:
            for part in range(2):
                rows = pl.ds(part * 128, 128)
                wait(pair_recv.at[m, block, :, rows, :], r["cr_sem"].at[m, block, part])

    def value_of(m, block, half):
        if WIDTH[m] == 128:
            return pair_keep[m, block, half] + pair_recv[m, block, half].astype(F32)
        return product(m, block, half)

    def ring_send(m, slot, value, dst, step):
        dws[m][slot] = value.astype(BF16)
        send(dws[m].at[slot], dst, r["rs_sem"].at[m, slot], r["rr_sem"].at[m, slot], device(dx=step))

    def send_across(m):
        wait_pair(m, across)
        for half, step in ((0, 1), (1, -1)):
            ring_send(m, half, value_of(m, across, half), relay[m].at[half], step)

    def send_near(m):
        wait_pair(m, before)
        wait_pair(m, after)
        for half, step, block in ((0, -1, before), (1, 1, after)):
            ring_send(m, 2 + half, value_of(m, block, half), near[m].at[half], step)

    def send_far(m):
        for half, step, block in ((0, 1, after), (1, -1, before)):
            value = value_of(m, block, half)
            wait(relay[m].at[half], r["rr_sem"].at[m, half])
            ring_send(m, 4 + half, value + relay[m][half].astype(F32), far[m].at[half], step)

    def keep(m):
        wait_pair(m, x)
        for half in range(2):
            own[m][half] = value_of(m, x, half)

    def across_y(m):
        for half in range(2):
            wait(near[m].at[half], r["rr_sem"].at[m, 2 + half])
            wait(far[m].at[half], r["rr_sem"].at[m, 4 + half])

        def total(half):
            return own[m][half] + near[m][half].astype(F32) + far[m][half].astype(F32)

        ysend[m][...] = total(1 - y_hi).astype(BF16)
        send(ysend[m], yrecv[m], r["ys_sem"].at[m], r["yr_sem"].at[m], device(dy=2))
        own[m][y_hi] = total(y_hi)

    zs_sem, zr_sem = r["zs_sem"], r["zr_sem"]

    def owner_copy(m, i):
        to_z = i if WIDTH[m] == 256 else odd * 8 + i
        slot = z if WIDTH[m] == 256 else lax.div(z, 2)
        copy = pltpu.make_async_remote_copy(
            src_ref=zsend[m].at[i], dst_ref=zrecv[m].at[slot], send_sem=zs_sem.at[m, i],
            recv_sem=zr_sem.at[m, slot], device_id=device(dz=to_z - z), device_id_type=MESH,
        )
        return to_z, copy

    def from_z(m, i):
        return i if WIDTH[m] == 256 else 2 * i + lax.div(z, 8)

    def across_z(m):
        wait(yrecv[m], r["yr_sem"].at[m])
        total = own[m][y_hi] + yrecv[m][...].astype(F32)
        zsend[m][...] = total.T.astype(BF16).reshape(WIDTH[m] // 16, 16, HK)

        def post(i, carry):
            to_z, copy = owner_copy(m, i)

            @pl.when(to_z != z)
            def _():
                copy.start()

            @pl.when(to_z == z)
            def _():
                slot = z if WIDTH[m] == 256 else lax.div(z, 2)
                zrecv[m][slot] = zsend[m][i]

            return carry

        lax.fori_loop(0, WIDTH[m] // 16, post, 0)

    def owned(m):
        def arrive(i, carry):
            @pl.when(from_z(m, i) != z)
            def _():
                wait(zrecv[m].at[i], zr_sem.at[m, i])

            return carry

        lax.fori_loop(0, WIDTH[m] // 16, arrive, 0)
        total = zrecv[m][0].astype(F32)
        for i in range(1, WIDTH[m] // 16):
            total = total + zrecv[m][i].astype(F32)
        return total * (1.0 / 256.0)

    def input_grad(b, carry):
        columns = aligned(b, Q)
        block, half = lax.div(b, 2), lax.rem(b, 2)
        rows = aligned(half, Q)
        total = lax.dot_general(gn[0], w[0, block, rows, :], NT, preferred_element_type=F32)
        total += lax.dot_general(gn[1], w[1, block, rows, :], NT, preferred_element_type=F32)

        @pl.when(core == 0)
        def _():
            igk[0, :, columns] = total[0:128]
            igk[1, :, columns] = total[256:384]
            igs[0, :, columns] = total[384:512].astype(BF16)
            igs[1, :, columns] = total[128:256].astype(BF16)

        @pl.when(core == 1)
        def _():
            igk[0, :, columns] = total[384:512]
            igk[1, :, columns] = total[128:256]
            igs[0, :, columns] = total[0:128].astype(BF16)
            igs[1, :, columns] = total[256:384].astype(BF16)

        return carry

    send_across(0)
    pair(1, across)
    pair(1, before)
    pair(1, after)
    send_near(0)
    pair(1, x)
    for block in (across, before, after, x):
        pair(2, block)
    send_far(0)
    keep(0)
    send_across(1)
    send_near(1)
    lax.fori_loop(0, 4, input_grad, 0)
    send_far(1)
    across_y(0)
    send_across(2)
    send_near(2)
    keep(1)
    lax.fori_loop(4, 8, input_grad, 0)
    send(igs, igr, r["is_sem"].at[0], r["ir_sem"].at[0], device(at=other))
    across_z(0)
    send_far(2)
    keep(2)
    across_y(1)
    wait(igr, r["ir_sem"].at[0])
    for slot in (1, 0):
        igo[slot] = (igk[slot] + igr[slot].astype(F32)).astype(BF16)
    send(igo.at[1], ig_hbm.at[:, mine], r["is_sem"].at[1], r["ir_sem"].at[1], device(dy=-side))
    done = pltpu.make_async_copy(igo.at[0], ig_hbm.at[:, mine], local_sem.at[3])
    done.start()
    across_z(1)
    across_y(2)
    across_z(2)

    for m in range(3):
        final = owned(m)

        @pl.when(core == 0)
        def _():
            wg_ref[m, :, 0:HK] = final[0:8]
            fsend[m] = final[8:16]

        @pl.when(core == 1)
        def _():
            wg_ref[m, :, HK : 2 * HK] = final[8:16]
            fsend[m] = final[0:8]

    send(fsend, frecv, r["fs_sem"], r["fr_sem"], device(at=other))
    wait(frecv, r["fr_sem"])

    @pl.when(core == 0)
    def _():
        wg_ref[:, :, HK : 2 * HK] = frecv[...]

    @pl.when(core == 1)
    def _():
        wg_ref[:, :, 0:HK] = frecv[...]

    done.wait()
    wait(ig_hbm.at[:, theirs], r["ir_sem"].at[1])
    for m in range(3):

        def left(i, carry):
            to_z, copy = owner_copy(m, i)

            @pl.when(to_z != z)
            def _():
                copy.wait_send()

            return carry

        lax.fori_loop(0, WIDTH[m] // 16, left, 0)
    for src, sem in sent:
        wait(src, sem)


def local(tokens, grad_out, quant_weights, block_scales):
    any_space = pl.BlockSpec(memory_space=pl.ANY)
    vmem = pl.BlockSpec(memory_space=pltpu.VMEM)
    return pl.pallas_call(
        kernel,
        out_shape=(
            jax.ShapeDtypeStruct((TOK, 2 * HALF), BF16),
            jax.ShapeDtypeStruct((3, 8, 2 * HK), F32),
        ),
        in_specs=[any_space, any_space, any_space, vmem],
        out_specs=(any_space, vmem),
        scratch_shapes=list(scratch().values()),
        compiler_params=pltpu.CompilerParams(
            collective_id=0, has_side_effects=True, vmem_limit_bytes=56 * 1024 * 1024
        ),
    )(tokens, grad_out, quant_weights, block_scales)


def solution(mesh):
    return jax.shard_map(
        local,
        mesh=mesh,
        in_specs=(
            P(("inner", "outer"), None),
            P(("inner", "outer"), None),
            P(None, "inner", None, None),
            P(None, "inner", None),
        ),
        out_specs=(P(("inner", "outer"), None), P(None, ("inner", "outer"), None)),
        check_vma=False,
    )
```

```python
import jax
import jax.numpy as jnp
from jax import lax
from jax.experimental import pallas as pl
from jax.experimental.pallas import tpu as pltpu
from jax.sharding import PartitionSpec as P

MESH = pl.DeviceIdType.MESH
BF16, F32 = jnp.bfloat16, jnp.float32
NX, NY, NZ = 4, 4, 16
TOK = 128
HALF = 2048
HK = 256
Q = 256
WIDTH = (256, 128, 128)
NT = (((1,), (1,)), ((), ()))


def scratch():
    vmem, dma = pltpu.VMEM, pltpu.SemaphoreType.DMA
    shapes = {
        "xt": vmem((4 * TOK, HALF), BF16),
        "xg": vmem((4 * TOK, HALF), BF16),
        "away": vmem((2, TOK, HALF), BF16),
        "quant": vmem((3, 4, 128, HK), BF16),
        "w": vmem((3, NX, 512, HK), BF16),
        "pacc": vmem((3, 4 * TOK, HK), F32),
        "psend": vmem((3, 4 * TOK, HK), BF16),
        "precv": vmem((3, 4 * TOK, HK), BF16),
        "gn": vmem((2, 4 * TOK, HK), BF16),
        "gt": vmem((3, HK, 4 * TOK), BF16),
        "pair_keep": vmem((3, NX, 2, HK, 128), F32),
        "pair_send": vmem((3, NX, 2, HK, 128), BF16),
        "pair_recv": vmem((3, NX, 2, HK, 128), BF16),
        "early_send": vmem((3, NX, HK, 128), BF16),
        "early_recv": vmem((3, NX, HK, 128), BF16),
        "igk": vmem((2, TOK, HALF), F32),
        "igs": vmem((2, TOK, HALF), BF16),
        "igr": vmem((2, TOK, HALF), BF16),
        "igo": vmem((2, TOK, HALF), BF16),
        "local_sem": dma((6,)),
        "xs_sem": dma((2, 5)), "xr_sem": dma((2, 5)),
        "ws_sem": dma((3, 10)), "wr_sem": dma((3, 10)),
        "ps_sem": dma((3, 2)), "pr_sem": dma((3, 2)),
        "cs_sem": dma((3, NX, 2)), "cr_sem": dma((3, NX, 2)),
        "rs_sem": dma((3, 6)), "rr_sem": dma((3, 6)),
        "es_sem": dma((3, NX)), "er_sem": dma((3, NX)),
        "ys_sem": dma, "yr_sem": dma,
        "zs_sem": dma((3, 2)), "zr_sem": dma((3, NZ)),
        "is_sem": dma((2,)), "ir_sem": dma((2,)),
    }
    shapes |= {"ysend": vmem((HK, Q), BF16), "yrecv": vmem((HK, Q), BF16)}
    for m, width in enumerate(WIDTH):
        piece = (width, width)
        shapes |= {
            f"dws{m}": vmem((6, *piece), BF16),
            f"own{m}": vmem((2, *piece), F32),
            f"relay{m}": vmem((2, *piece), BF16),
            f"near{m}": vmem((2, *piece), BF16),
            f"far{m}": vmem((2, *piece), BF16),
            f"zsend{m}": vmem((width // 16, 2, 16, 128), BF16),
            f"zrecv{m}": vmem((width // 16, 2, 16, 128), BF16),
        }
    return shapes


def aligned(index, size):
    return pl.ds(pl.multiple_of(index * size, size), size)


def dot(a, b):
    return jnp.dot(a, b, preferred_element_type=F32)


def kernel(tok_hbm, out_hbm, quant_hbm, scales, ig_hbm, wg_ref, *scratch_refs):
    r = dict(zip(scratch(), scratch_refs, strict=True))
    xt, xg, away, quant, w, pacc, psend, precv, gn, gt = (
        r[name] for name in ("xt", "xg", "away", "quant", "w", "pacc", "psend", "precv", "gn", "gt")
    )
    pair_keep, pair_send, pair_recv = r["pair_keep"], r["pair_send"], r["pair_recv"]
    igk, igs, igr, igo = (r[name] for name in ("igk", "igs", "igr", "igo"))
    local_sem, xs_sem, xr_sem, ws_sem, wr_sem = (
        r[name] for name in ("local_sem", "xs_sem", "xr_sem", "ws_sem", "wr_sem")
    )
    dws, own, relay, near, far, zsend, zrecv = (
        [r[f"{name}{m}"] for m in range(3)]
        for name in ("dws", "own", "relay", "near", "far", "zsend", "zrecv")
    )
    ysend, yrecv, early_send, early_recv = (
        r[name] for name in ("ysend", "yrecv", "early_send", "early_recv")
    )

    inner, outer = lax.axis_index("inner"), lax.axis_index("outer")
    x, y_lo = lax.rem(inner, NX), lax.div(inner, NX)
    core, z = lax.rem(outer, 2), lax.rem(lax.div(outer, 2), NZ)
    y_hi = lax.div(outer, 2 * NZ)
    y = 2 * y_hi + y_lo
    other = 1 - core
    odd = lax.rem(z, 2)
    before, after, across = (lax.rem(x + step, NX) for step in (3, 1, 2))

    def device(dx=0, dy=0, dz=0, at=core):
        to_x, to_y, to_z = (
            lax.rem(x + dx + NX, NX),
            lax.rem(y + dy + NY, NY),
            lax.rem(z + dz + NZ, NZ),
        )
        return (
            lax.rem(to_y, 2) * NX + to_x,
            (lax.div(to_y, 2) * NZ + to_z) * 2 + at,
        )

    sent = []

    def drain(count):
        for src, sem in sent[:count]:
            wait(src, sem)
        del sent[:count]

    def send(src, dst, s_sem, r_sem, to):
        pltpu.make_async_remote_copy(
            src_ref=src, dst_ref=dst, send_sem=s_sem, recv_sem=r_sem, device_id=to, device_id_type=MESH
        ).start()
        sent.append((src, s_sem))

    def wait(ref, sem):
        pltpu.make_async_copy(ref, ref, sem).wait()

    side = 1 - 2 * core
    mine, theirs = aligned(y_lo, HALF), aligned(1 - y_lo, HALF)
    hidden_half = aligned(core, HK)

    own_rows = aligned(3 * core, TOK)
    pltpu.make_async_copy(quant_hbm.at[:, :, :, hidden_half], quant, local_sem.at[0]).start()
    pltpu.make_async_copy(tok_hbm.at[:, mine], xt.at[own_rows, :], local_sem.at[1]).start()
    pltpu.make_async_copy(out_hbm.at[:, mine], xg.at[own_rows, :], local_sem.at[2]).start()
    pltpu.make_async_copy(tok_hbm.at[:, theirs], away.at[0], local_sem.at[3]).start()
    pltpu.make_async_copy(out_hbm.at[:, theirs], away.at[1], local_sem.at[4]).start()

    barrier = pltpu.get_barrier_semaphore()
    partners = [
        device(at=other), device(dx=1), device(dx=-1), device(dy=1), device(dy=-1), device(dy=2),
        device(dy=side, at=other),
    ]
    column = outer - 2 * z - core
    for j in sorted(range(1, NZ), key=lambda j: -min(j, NZ - j)):
        for at in range(2):
            to = column + 2 * ((z + j) & (NZ - 1)) + at
            pl.semaphore_signal(barrier, inc=1, device_id=(inner, to), device_id_type=MESH)
    for to in partners:
        pl.semaphore_signal(barrier, inc=1, device_id=to, device_id_type=MESH)

    def dequantise(m):
        for b in range(4):
            scale = scales[m, pl.ds(b, 1), hidden_half]
            w[m, x, b * 128 : (b + 1) * 128, :] = (quant[m, b].astype(F32) * scale).astype(BF16)

    wait(quant, local_sem.at[0])
    dequantise(0)
    pl.semaphore_wait(barrier, len(partners) + 2 * (NZ - 1))

    def send_tokens(a, dst):
        wait(away.at[a], local_sem.at[3 + a])
        for part in range(2):
            rows = pl.ds(part * 64, 64)
            to_rows = pl.ds(pl.multiple_of((2 - core) * TOK + part * 64, 64), 64)
            send(
                away.at[a, rows, :], dst.at[to_rows, :], xs_sem.at[a, part], xr_sem.at[a, core],
                device(dy=side, at=part),
            )
        wait(dst.at[own_rows, :], local_sem.at[1 + a])
        send(dst.at[own_rows, :], dst.at[own_rows, :], xs_sem.at[a, 2], xr_sem.at[a, 2], device(at=other))

    def pass_tokens(a, dst):
        for i, block in enumerate((2, 1)):
            rows = pl.ds(pl.multiple_of(block * TOK + core * 64, 64), 64)
            wait(dst.at[rows, :], xr_sem.at[a, i])
            send(dst.at[rows, :], dst.at[rows, :], xs_sem.at[a, 3 + i], xr_sem.at[a, 3 + i], device(at=other))

    def wait_tokens(a, dst):
        wait(dst.at[aligned(3 - 3 * core, TOK), :], xr_sem.at[a, 2])
        for i, block in enumerate((2, 1)):
            rows = pl.ds(pl.multiple_of(block * TOK + other * 64, 64), 64)
            wait(dst.at[rows, :], xr_sem.at[a, 3 + i])

    def quarter(m, shard, half, q):
        return w.at[m, shard, pl.ds(pl.multiple_of(half * 256 + q * 128, 128), 128), :]

    def half_of(m, shard):
        return w.at[m, shard, aligned(odd, 256), :]

    def pass_on(m, ref, channel, to):
        send(ref, ref, ws_sem.at[m, channel], wr_sem.at[m, channel], to)

    def send_weights(m):
        pass_on(m, half_of(m, x), 0, device(dx=1))
        pass_on(m, half_of(m, x), 1, device(dx=-1))

    def relay_weights(m):
        for i, (shard, step) in enumerate(((before, 1), (after, -1))):
            wait(half_of(m, shard), wr_sem.at[m, i])
            pass_on(m, quarter(m, shard, odd, i), 2 + i, device(dx=step))
            pass_on(m, quarter(m, shard, odd, 0), 4 + 2 * i, device(dz=1))
            pass_on(m, quarter(m, shard, odd, 1), 5 + 2 * i, device(dz=-1))

    def relay_across(m):
        for q, step in ((0, 1), (1, -1)):
            wait(quarter(m, across, odd, q), wr_sem.at[m, 2 + q])
            pass_on(m, quarter(m, across, odd, q), 8 + q, device(dz=step))

    def term(m, shard, half):
        columns = aligned(shard * 2 + half, 256)
        return dot((xg if m == 2 else xt)[:, columns], w[m, shard, aligned(half, 256), :])

    def first_terms(m):
        pacc[m] = term(m, x, 0) + term(m, x, 1) + term(m, before, odd) + term(m, after, odd)

    def last_terms(m):
        for i, shard in enumerate((before, after, across)):
            for q in range(2):
                wait(quarter(m, shard, 1 - odd, q), wr_sem.at[m, 4 + 2 * i + q])
        total = (
            pacc[m] + term(m, before, 1 - odd) + term(m, after, 1 - odd)
            + term(m, across, 0) + term(m, across, 1)
        )
        pacc[m] = total
        psend[m] = total.astype(BF16)
        low, high = pl.ds(0, 256), pl.ds(256, 256)
        send(psend.at[m, low], precv.at[m, high], r["ps_sem"].at[m, 0], r["pr_sem"].at[m, 0], device(dy=1))
        send(psend.at[m, high], precv.at[m, low], r["ps_sem"].at[m, 1], r["pr_sem"].at[m, 1], device(dy=-1))

    send_weights(0)
    send_tokens(0, xt)
    dequantise(1)
    send_weights(1)
    send_tokens(1, xg)
    dequantise(2)
    relay_weights(0)
    send_weights(2)
    relay_weights(1)
    relay_across(0)
    pass_tokens(0, xt)
    relay_weights(2)
    relay_across(1)
    wait_tokens(0, xt)
    first_terms(0)
    last_terms(0)
    relay_across(2)
    first_terms(1)
    pass_tokens(1, xg)
    last_terms(1)
    wait_tokens(1, xg)
    first_terms(2)
    last_terms(2)

    for m in range(3):
        wait(precv.at[m, pl.ds(256, 256)], r["pr_sem"].at[m, 0])
        wait(precv.at[m, pl.ds(0, 256)], r["pr_sem"].at[m, 1])

    def elementwise(b, carry):
        rows = aligned(b, 128)
        gate, up, d_hidden = (pacc[m, rows, :] + precv[m, rows, :].astype(F32) for m in range(3))
        s = jax.nn.sigmoid(gate)
        hidden = (gate * s * up).astype(BF16)
        grad_up = (d_hidden * gate * s).astype(BF16)
        grad_gate = (d_hidden * up * s * (1.0 + gate * (1.0 - s))).astype(BF16)
        gn[0, rows, :] = grad_gate
        gn[1, rows, :] = grad_up
        gt[0, :, rows] = grad_gate.T
        gt[1, :, rows] = grad_up.T
        gt[2, :, rows] = hidden.T
        return carry

    lax.fori_loop(0, 4, elementwise, 0)

    def product(m, block, half):
        return dot(gt[m], (xg if m == 2 else xt)[:, aligned(block * 2 + half, Q)])

    def pair(m, block):
        for half in range(2):
            value = product(m, block, half)
            low, high = value[:, :128], value[:, 128:]
            pair_keep[m, block, half] = jnp.where(odd == 0, low, high)
            pair_send[m, block, half] = jnp.where(odd == 0, high, low).astype(BF16)
        for part, step in ((0, 1), (1, -1)):
            rows = pl.ds(part * 128, 128)
            send(
                pair_send.at[m, block, :, rows, :], pair_recv.at[m, block, :, rows, :],
                r["cs_sem"].at[m, block, part], r["cr_sem"].at[m, block, part], device(dz=step),
            )

    def swap_y(m, block):
        for part in range(2):
            rows = pl.ds(part * 128, 128)
            wait(pair_recv.at[m, block, :, rows, :], r["cr_sem"].at[m, block, part])
        gone = 1 - y_hi
        early_send[m, block] = (
            pair_keep[m, block, gone] + pair_recv[m, block, gone].astype(F32)
        ).astype(BF16)
        send(
            early_send.at[m, block], early_recv.at[m, block], r["es_sem"].at[m, block], r["er_sem"].at[m, block],
            device(dy=2),
        )

    def wait_block(m, block):
        if WIDTH[m] == 128:
            wait(early_recv.at[m, block], r["er_sem"].at[m, block])

    def value_of(m, block, half):
        if WIDTH[m] == 128:
            rows = pl.ds(half * 128, 128)
            return (
                pair_keep[m, block, y_hi, rows, :]
                + pair_recv[m, block, y_hi, rows, :].astype(F32)
                + early_recv[m, block, rows, :].astype(F32)
            )
        return product(m, block, half)

    def ring_send(m, slot, value, dst, step):
        dws[m][slot] = value.astype(BF16)
        send(dws[m].at[slot], dst, r["rs_sem"].at[m, slot], r["rr_sem"].at[m, slot], device(dx=step))

    def send_across(m):
        wait_block(m, across)
        for half, step in ((0, 1), (1, -1)):
            ring_send(m, half, value_of(m, across, half), relay[m].at[half], step)

    def send_near(m):
        wait_block(m, before)
        wait_block(m, after)
        for half, step, block in ((0, -1, before), (1, 1, after)):
            ring_send(m, 2 + half, value_of(m, block, half), near[m].at[half], step)

    def send_far(m):
        for half, step, block in ((0, 1, after), (1, -1, before)):
            value = value_of(m, block, half)
            wait(relay[m].at[half], r["rr_sem"].at[m, half])
            ring_send(m, 4 + half, value + relay[m][half].astype(F32), far[m].at[half], step)

    def keep(m):
        wait_block(m, x)
        for half in range(2):
            own[m][half] = value_of(m, x, half)

    def total_of(m, half):
        return own[m][half] + near[m][half].astype(F32) + far[m][half].astype(F32)

    def wait_ring(m):
        for half in range(2):
            wait(near[m].at[half], r["rr_sem"].at[m, 2 + half])
            wait(far[m].at[half], r["rr_sem"].at[m, 4 + half])

    def across_y(m):
        wait_ring(m)
        ysend[...] = total_of(m, 1 - y_hi).astype(BF16)
        send(ysend, yrecv, r["ys_sem"], r["yr_sem"], device(dy=2))
        own[m][y_hi] = total_of(m, y_hi)

    zs_sem, zr_sem = r["zs_sem"], r["zr_sem"]

    def owner_of(m, i):
        if WIDTH[m] == 256:
            return i, z
        return odd * 8 + i, lax.div(z, 2)

    def across_z(m):
        if WIDTH[m] == 128:
            wait_ring(m)
            total = jnp.concatenate([total_of(m, 0), total_of(m, 1)]).T
        else:
            wait(yrecv, r["yr_sem"])
            total = (own[m][y_hi] + yrecv[...].astype(F32)).T
        for i in range(WIDTH[m] // 16):
            for to in range(2):
                rows = total[16 * i + 8 * to : 16 * i + 8 * to + 8]
                zsend[m][i, to] = jnp.concatenate([rows[:, :128], rows[:, 128:]]).astype(BF16)

        def post(i, carry):
            to_z, slot = owner_of(m, i)

            def copy(to, sem):
                pltpu.make_async_remote_copy(
                    src_ref=zsend[m].at[i, to], dst_ref=zrecv[m].at[slot, core], send_sem=zs_sem.at[m, sem],
                    recv_sem=zr_sem.at[m, slot], device_id=device(dz=to_z - z, at=to), device_id_type=MESH,
                ).start()

            @pl.when(to_z != z)
            def _():
                copy(0, 0)
                copy(1, 0)

            @pl.when(to_z == z)
            def _():
                copy(other, 1)
                zrecv[m][slot, core] = zsend[m][i, core]

            return carry

        lax.fori_loop(0, WIDTH[m] // 16, post, 0)

    def owned(m):
        count = WIDTH[m] // 16

        def arrive(i, carry):
            from_z = i if count == NZ else 2 * i + lax.div(z, 8)

            @pl.when(from_z != z)
            def _():
                wait(zrecv[m].at[i], zr_sem.at[m, i])

            @pl.when(from_z == z)
            def _():
                wait(zrecv[m].at[i, other], zr_sem.at[m, i])

            return carry

        lax.fori_loop(0, count, arrive, 0)
        for half in range(2):
            total = zrecv[m][0, half].astype(F32)
            for i in range(1, count):
                total = total + zrecv[m][i, half].astype(F32)
            total = total * (1.0 / 256.0)
            for part in range(2):
                first = half * HK + part * 128
                wg_ref[m, :, first : first + 128] = total[8 * part : 8 * part + 8]

    def left(m):
        count = WIDTH[m] // 16
        to_self = (odd * 8 <= z) & (z < odd * 8 + 8)
        if count == NZ:
            wait(zsend[m].at[pl.ds(0, NZ - 1)], zs_sem.at[m, 0])
            wait(zsend[m].at[0, 0], zs_sem.at[m, 1])
            return

        @pl.when(to_self)
        def _():
            wait(zsend[m].at[pl.ds(0, count - 1)], zs_sem.at[m, 0])
            wait(zsend[m].at[0, 0], zs_sem.at[m, 1])

        @pl.when(jnp.logical_not(to_self))
        def _():
            wait(zsend[m], zs_sem.at[m, 0])

    def input_grad(b, carry):
        columns = aligned(b, Q)
        block, half = lax.div(b, 2), lax.rem(b, 2)
        rows = aligned(half, Q)
        total = lax.dot_general(gn[0], w[0, block, rows, :], NT, preferred_element_type=F32)
        total += lax.dot_general(gn[1], w[1, block, rows, :], NT, preferred_element_type=F32)

        @pl.when(core == 0)
        def _():
            igk[0, :, columns] = total[0:128]
            igk[1, :, columns] = total[256:384]
            igs[0, :, columns] = total[384:512].astype(BF16)
            igs[1, :, columns] = total[128:256].astype(BF16)

        @pl.when(core == 1)
        def _():
            igk[0, :, columns] = total[384:512]
            igk[1, :, columns] = total[128:256]
            igs[0, :, columns] = total[0:128].astype(BF16)
            igs[1, :, columns] = total[256:384].astype(BF16)

        return carry

    early = len(sent)
    order = (across, before, after, x)
    send_across(0)
    send_near(0)
    for m in (1, 2):
        for block in order:
            pair(m, block)
    lax.fori_loop(0, 5, input_grad, 0)
    swap_y(1, across)
    swap_y(1, before)
    send_far(0)
    lax.fori_loop(5, 8, input_grad, 0)
    send(igs, igr, r["is_sem"].at[0], r["ir_sem"].at[0], device(at=other))
    swap_y(1, after)
    swap_y(1, x)
    keep(0)
    drain(early)
    send_across(1)
    across_y(0)
    swap_y(2, across)
    swap_y(2, before)
    send_near(1)
    keep(1)
    send_far(1)
    swap_y(2, after)
    swap_y(2, x)
    send_across(2)
    across_z(1)
    send_near(2)
    across_z(0)
    wait(igr, r["ir_sem"].at[0])
    for slot in (1, 0):
        igo[slot] = (igk[slot] + igr[slot].astype(F32)).astype(BF16)
    send(igo.at[1], ig_hbm.at[:, mine], r["is_sem"].at[1], r["ir_sem"].at[1], device(dy=-side))
    done = pltpu.make_async_copy(igo.at[0], ig_hbm.at[:, mine], local_sem.at[5])
    done.start()
    drain(len(sent) - 1)
    send_far(2)
    keep(2)
    across_z(2)
    owned(1)
    left(1)
    owned(0)
    left(0)
    done.wait()
    wait(ig_hbm.at[:, theirs], r["ir_sem"].at[1])
    drain(len(sent))
    left(2)
    owned(2)


def local(tokens, grad_out, quant_weights, block_scales):
    any_space = pl.BlockSpec(memory_space=pl.ANY)
    vmem = pl.BlockSpec(memory_space=pltpu.VMEM)
    return pl.pallas_call(
        kernel,
        out_shape=(
            jax.ShapeDtypeStruct((TOK, 2 * HALF), BF16),
            jax.ShapeDtypeStruct((3, 8, 2 * HK), F32),
        ),
        in_specs=[any_space, any_space, any_space, vmem],
        out_specs=(any_space, vmem),
        scratch_shapes=list(scratch().values()),
        compiler_params=pltpu.CompilerParams(
            collective_id=0, has_side_effects=True, vmem_limit_bytes=56 * 1024 * 1024
        ),
    )(tokens, grad_out, quant_weights, block_scales)


def solution(mesh):
    return jax.shard_map(
        local,
        mesh=mesh,
        in_specs=(
            P(("inner", "outer"), None),
            P(("inner", "outer"), None),
            P(None, "inner", None, None),
            P(None, "inner", None),
        ),
        out_specs=(P(("inner", "outer"), None), P(None, ("inner", "outer"), None)),
        check_vma=False,
    )
```

```python
import jax
import jax.numpy as jnp
from jax import lax
from jax.experimental import pallas as pl
from jax.experimental.pallas import tpu as pltpu
from jax.sharding import PartitionSpec as P

MESH = pl.DeviceIdType.MESH
BF16, F32 = jnp.bfloat16, jnp.float32
NX, NY, NZ = 4, 4, 16
TOK = 128
HALF = 2048
HK = 256
Q = 256
WIDTH = (256, 128, 128)
EARLY = (False, True, True)
NT = (((1,), (1,)), ((), ()))


def scratch():
    vmem, dma = pltpu.VMEM, pltpu.SemaphoreType.DMA
    shapes = {
        "xt": vmem((4 * TOK, HALF), BF16),
        "xg": vmem((4 * TOK, HALF), BF16),
        "away": vmem((2, TOK, HALF), BF16),
        "quant": vmem((3, 4, 128, HK), BF16),
        "w": vmem((3, NX, 512, HK), BF16),
        "pacc": vmem((3, 4 * TOK, HK), F32),
        "psend": vmem((3, 4 * TOK, HK), BF16),
        "precv": vmem((3, 4 * TOK, HK), BF16),
        "gn": vmem((2, 4 * TOK, HK), BF16),
        "gt": vmem((3, HK, 4 * TOK), BF16),
        "pair_keep": vmem((3, NX, 2, HK, 128), F32),
        "pair_send": vmem((3, NX, 2, HK, 128), BF16),
        "pair_recv": vmem((3, NX, 2, HK, 128), BF16),
        "early_send": vmem((3, NX, HK, 128), BF16),
        "early_recv": vmem((3, NX, HK, 128), BF16),
        "igk": vmem((2, TOK, HALF), F32),
        "igs": vmem((2, TOK, HALF), BF16),
        "igr": vmem((2, TOK, HALF), BF16),
        "igo": vmem((2, TOK, HALF), BF16),
        "local_sem": dma((6,)),
        "xs_sem": dma((2, 5)), "xr_sem": dma((2, 5)),
        "ws_sem": dma((3, 10)), "wr_sem": dma((3, 10)),
        "ps_sem": dma((3, 2)), "pr_sem": dma((3, 2)),
        "cs_sem": dma((3, NX, 2)), "cr_sem": dma((3, NX, 2)),
        "rs_sem": dma((3, 6)), "rr_sem": dma((3, 6)),
        "es_sem": dma((3, NX)), "er_sem": dma((3, NX)),
        "ys_sem": dma((3,)), "yr_sem": dma((3,)),
        "zs_sem": dma((3, 2)), "zr_sem": dma((3, NZ)),
        "is_sem": dma((2,)), "ir_sem": dma((2,)),
    }
    for m, width in enumerate(WIDTH):
        piece = (128 if EARLY[m] else 256, width)
        shapes |= {
            f"dws{m}": vmem((6, *piece), BF16),
            f"own{m}": vmem((2, *piece), F32),
            f"relay{m}": vmem((2, *piece), BF16),
            f"near{m}": vmem((2, *piece), BF16),
            f"far{m}": vmem((2, *piece), BF16),
            f"ysend{m}": vmem(piece, BF16),
            f"yrecv{m}": vmem(piece, BF16),
            f"zsend{m}": vmem((width // 16, 2, 16, 128), BF16),
            f"zrecv{m}": vmem((width // 16, 2, 16, 128), BF16),
        }
    return shapes


def aligned(index, size):
    return pl.ds(pl.multiple_of(index * size, size), size)


def dot(a, b):
    return jnp.dot(a, b, preferred_element_type=F32)


def kernel(tok_hbm, out_hbm, quant_hbm, scales, ig_hbm, wg_ref, *scratch_refs):
    r = dict(zip(scratch(), scratch_refs, strict=True))
    xt, xg, away, quant, w, pacc, psend, precv, gn, gt = (
        r[name] for name in ("xt", "xg", "away", "quant", "w", "pacc", "psend", "precv", "gn", "gt")
    )
    pair_keep, pair_send, pair_recv = r["pair_keep"], r["pair_send"], r["pair_recv"]
    igk, igs, igr, igo = (r[name] for name in ("igk", "igs", "igr", "igo"))
    local_sem, xs_sem, xr_sem, ws_sem, wr_sem = (
        r[name] for name in ("local_sem", "xs_sem", "xr_sem", "ws_sem", "wr_sem")
    )
    dws, own, relay, near, far, ysend, yrecv, zsend, zrecv = (
        [r[f"{name}{m}"] for m in range(3)]
        for name in ("dws", "own", "relay", "near", "far", "ysend", "yrecv", "zsend", "zrecv")
    )
    early_send, early_recv = r["early_send"], r["early_recv"]

    inner, outer = lax.axis_index("inner"), lax.axis_index("outer")
    x, y_lo = lax.rem(inner, NX), lax.div(inner, NX)
    core, z = lax.rem(outer, 2), lax.rem(lax.div(outer, 2), NZ)
    y_hi = lax.div(outer, 2 * NZ)
    y = 2 * y_hi + y_lo
    other = 1 - core
    odd = lax.rem(z, 2)
    before, after, across = (lax.rem(x + step, NX) for step in (3, 1, 2))

    def device(dx=0, dy=0, dz=0, at=core):
        to_x, to_y, to_z = (
            lax.rem(x + dx + NX, NX),
            lax.rem(y + dy + NY, NY),
            lax.rem(z + dz + NZ, NZ),
        )
        return (
            lax.rem(to_y, 2) * NX + to_x,
            (lax.div(to_y, 2) * NZ + to_z) * 2 + at,
        )

    sent = []

    def drain(count):
        for src, sem in sent[:count]:
            wait(src, sem)
        del sent[:count]

    def send(src, dst, s_sem, r_sem, to):
        pltpu.make_async_remote_copy(
            src_ref=src, dst_ref=dst, send_sem=s_sem, recv_sem=r_sem, device_id=to, device_id_type=MESH
        ).start()
        sent.append((src, s_sem))

    def wait(ref, sem):
        pltpu.make_async_copy(ref, ref, sem).wait()

    side = 1 - 2 * core
    mine, theirs = aligned(y_lo, HALF), aligned(1 - y_lo, HALF)
    hidden_half = aligned(core, HK)

    own_rows = aligned(3 * core, TOK)
    pltpu.make_async_copy(quant_hbm.at[:, :, :, hidden_half], quant, local_sem.at[0]).start()
    pltpu.make_async_copy(tok_hbm.at[:, mine], xt.at[own_rows, :], local_sem.at[1]).start()
    pltpu.make_async_copy(out_hbm.at[:, mine], xg.at[own_rows, :], local_sem.at[2]).start()
    pltpu.make_async_copy(tok_hbm.at[:, theirs], away.at[0], local_sem.at[3]).start()
    pltpu.make_async_copy(out_hbm.at[:, theirs], away.at[1], local_sem.at[4]).start()

    barrier = pltpu.get_barrier_semaphore()
    partners = [
        device(at=other), device(dx=1), device(dx=-1), device(dy=1), device(dy=-1), device(dy=2),
        device(dy=side, at=other),
    ]
    column = outer - 2 * z - core
    for j in sorted(range(1, NZ), key=lambda j: -min(j, NZ - j)):
        for at in range(2):
            to = column + 2 * ((z + j) & (NZ - 1)) + at
            pl.semaphore_signal(barrier, inc=1, device_id=(inner, to), device_id_type=MESH)
    for to in partners:
        pl.semaphore_signal(barrier, inc=1, device_id=to, device_id_type=MESH)

    def dequantise(m):
        for b in range(4):
            scale = scales[m, pl.ds(b, 1), hidden_half]
            w[m, x, b * 128 : (b + 1) * 128, :] = (quant[m, b].astype(F32) * scale).astype(BF16)

    wait(quant, local_sem.at[0])
    dequantise(0)
    pl.semaphore_wait(barrier, len(partners) + 2 * (NZ - 1))

    def send_tokens(a, dst):
        wait(away.at[a], local_sem.at[3 + a])
        for part in range(2):
            rows = pl.ds(part * 64, 64)
            to_rows = pl.ds(pl.multiple_of((2 - core) * TOK + part * 64, 64), 64)
            send(
                away.at[a, rows, :], dst.at[to_rows, :], xs_sem.at[a, part], xr_sem.at[a, core],
                device(dy=side, at=part),
            )
        wait(dst.at[own_rows, :], local_sem.at[1 + a])
        send(dst.at[own_rows, :], dst.at[own_rows, :], xs_sem.at[a, 2], xr_sem.at[a, 2], device(at=other))

    def pass_tokens(a, dst):
        for i, block in enumerate((2, 1)):
            rows = pl.ds(pl.multiple_of(block * TOK + core * 64, 64), 64)
            wait(dst.at[rows, :], xr_sem.at[a, i])
            send(dst.at[rows, :], dst.at[rows, :], xs_sem.at[a, 3 + i], xr_sem.at[a, 3 + i], device(at=other))

    def wait_tokens(a, dst):
        wait(dst.at[aligned(3 - 3 * core, TOK), :], xr_sem.at[a, 2])
        for i, block in enumerate((2, 1)):
            rows = pl.ds(pl.multiple_of(block * TOK + other * 64, 64), 64)
            wait(dst.at[rows, :], xr_sem.at[a, 3 + i])

    def quarter(m, shard, half, q):
        return w.at[m, shard, pl.ds(pl.multiple_of(half * 256 + q * 128, 128), 128), :]

    def half_of(m, shard):
        return w.at[m, shard, aligned(odd, 256), :]

    def pass_on(m, ref, channel, to):
        send(ref, ref, ws_sem.at[m, channel], wr_sem.at[m, channel], to)

    def send_weights(m):
        pass_on(m, half_of(m, x), 0, device(dx=1))
        pass_on(m, half_of(m, x), 1, device(dx=-1))

    def relay_weights(m):
        for i, (shard, step) in enumerate(((before, 1), (after, -1))):
            wait(half_of(m, shard), wr_sem.at[m, i])
            pass_on(m, quarter(m, shard, odd, i), 2 + i, device(dx=step))
            pass_on(m, quarter(m, shard, odd, 0), 4 + 2 * i, device(dz=1))
            pass_on(m, quarter(m, shard, odd, 1), 5 + 2 * i, device(dz=-1))

    def relay_across(m):
        for q, step in ((0, 1), (1, -1)):
            wait(quarter(m, across, odd, q), wr_sem.at[m, 2 + q])
            pass_on(m, quarter(m, across, odd, q), 8 + q, device(dz=step))

    def term(m, shard, half):
        columns = aligned(shard * 2 + half, 256)
        return dot((xg if m == 2 else xt)[:, columns], w[m, shard, aligned(half, 256), :])

    def first_terms(m):
        pacc[m] = term(m, x, 0) + term(m, x, 1) + term(m, before, odd) + term(m, after, odd)

    def last_terms(m):
        for i, shard in enumerate((before, after, across)):
            for q in range(2):
                wait(quarter(m, shard, 1 - odd, q), wr_sem.at[m, 4 + 2 * i + q])
        total = (
            pacc[m] + term(m, before, 1 - odd) + term(m, after, 1 - odd)
            + term(m, across, 0) + term(m, across, 1)
        )
        pacc[m] = total
        psend[m] = total.astype(BF16)
        low, high = pl.ds(0, 256), pl.ds(256, 256)
        send(psend.at[m, low], precv.at[m, high], r["ps_sem"].at[m, 0], r["pr_sem"].at[m, 0], device(dy=1))
        send(psend.at[m, high], precv.at[m, low], r["ps_sem"].at[m, 1], r["pr_sem"].at[m, 1], device(dy=-1))

    send_weights(0)
    send_tokens(0, xt)
    dequantise(1)
    send_weights(1)
    send_tokens(1, xg)
    dequantise(2)
    relay_weights(0)
    send_weights(2)
    relay_weights(1)
    relay_across(0)
    pass_tokens(0, xt)
    relay_weights(2)
    relay_across(1)
    wait_tokens(0, xt)
    first_terms(0)
    last_terms(0)
    first_terms(1)
    relay_across(2)
    last_terms(1)
    pass_tokens(1, xg)
    wait_tokens(1, xg)
    first_terms(2)
    last_terms(2)

    def wait_partial(m):
        wait(precv.at[m, pl.ds(256, 256)], r["pr_sem"].at[m, 0])
        wait(precv.at[m, pl.ds(0, 256)], r["pr_sem"].at[m, 1])

    def elementwise_hidden(b, carry):
        rows = aligned(b, 128)
        gate, up = (pacc[m, rows, :] + precv[m, rows, :].astype(F32) for m in range(2))
        s = jax.nn.sigmoid(gate)
        pacc[0, rows, :] = gate * s
        pacc[1, rows, :] = up * s * (1.0 + gate * (1.0 - s))
        gt[2, :, rows] = (gate * s * up).astype(BF16).T
        return carry

    def elementwise_grads(b, carry):
        rows = aligned(b, 128)
        d_hidden = pacc[2, rows, :] + precv[2, rows, :].astype(F32)
        grad_up = (d_hidden * pacc[0, rows, :]).astype(BF16)
        grad_gate = (d_hidden * pacc[1, rows, :]).astype(BF16)
        gn[0, rows, :] = grad_gate
        gn[1, rows, :] = grad_up
        gt[0, :, rows] = grad_gate.T
        gt[1, :, rows] = grad_up.T
        return carry

    def product(m, block, half):
        return dot(gt[m], (xg if m == 2 else xt)[:, aligned(block * 2 + half, Q)])

    def pair(m, block):
        for half in range(2):
            value = product(m, block, half)
            low, high = value[:, :128], value[:, 128:]
            pair_keep[m, block, half] = jnp.where(odd == 0, low, high)
            pair_send[m, block, half] = jnp.where(odd == 0, high, low).astype(BF16)
        for part, step in ((0, 1), (1, -1)):
            rows = pl.ds(part * 128, 128)
            send(
                pair_send.at[m, block, :, rows, :], pair_recv.at[m, block, :, rows, :],
                r["cs_sem"].at[m, block, part], r["cr_sem"].at[m, block, part], device(dz=step),
            )

    def wait_pair(m, block):
        for part in range(2):
            rows = pl.ds(part * 128, 128)
            wait(pair_recv.at[m, block, :, rows, :], r["cr_sem"].at[m, block, part])

    def swap_y(m, block):
        wait_pair(m, block)
        gone = 1 - y_hi
        early_send[m, block] = (
            pair_keep[m, block, gone] + pair_recv[m, block, gone].astype(F32)
        ).astype(BF16)
        send(
            early_send.at[m, block], early_recv.at[m, block], r["es_sem"].at[m, block], r["er_sem"].at[m, block],
            device(dy=2),
        )

    def wait_block(m, block):
        if EARLY[m]:
            wait(early_recv.at[m, block], r["er_sem"].at[m, block])
        elif WIDTH[m] == 128:
            wait_pair(m, block)

    def value_of(m, block, half):
        if EARLY[m]:
            rows = pl.ds(half * 128, 128)
            return (
                pair_keep[m, block, y_hi, rows, :]
                + pair_recv[m, block, y_hi, rows, :].astype(F32)
                + early_recv[m, block, rows, :].astype(F32)
            )
        if WIDTH[m] == 128:
            return pair_keep[m, block, half] + pair_recv[m, block, half].astype(F32)
        return product(m, block, half)

    def ring_send(m, slot, value, dst, step):
        dws[m][slot] = value.astype(BF16)
        send(dws[m].at[slot], dst, r["rs_sem"].at[m, slot], r["rr_sem"].at[m, slot], device(dx=step))

    def send_across(m):
        wait_block(m, across)
        for half, step in ((0, 1), (1, -1)):
            ring_send(m, half, value_of(m, across, half), relay[m].at[half], step)

    def send_near(m):
        wait_block(m, before)
        wait_block(m, after)
        for half, step, block in ((0, -1, before), (1, 1, after)):
            ring_send(m, 2 + half, value_of(m, block, half), near[m].at[half], step)

    def send_far(m):
        for half, step, block in ((0, 1, after), (1, -1, before)):
            value = value_of(m, block, half)
            wait(relay[m].at[half], r["rr_sem"].at[m, half])
            ring_send(m, 4 + half, value + relay[m][half].astype(F32), far[m].at[half], step)

    def keep(m):
        wait_block(m, x)
        for half in range(2):
            own[m][half] = value_of(m, x, half)

    def total_of(m, half):
        return own[m][half] + near[m][half].astype(F32) + far[m][half].astype(F32)

    def wait_ring(m):
        for half in range(2):
            wait(near[m].at[half], r["rr_sem"].at[m, 2 + half])
            wait(far[m].at[half], r["rr_sem"].at[m, 4 + half])

    def across_y(m):
        wait_ring(m)
        ysend[m][...] = total_of(m, 1 - y_hi).astype(BF16)
        send(ysend[m], yrecv[m], r["ys_sem"].at[m], r["yr_sem"].at[m], device(dy=2))
        own[m][y_hi] = total_of(m, y_hi)

    zs_sem, zr_sem = r["zs_sem"], r["zr_sem"]

    def owner_of(m, i):
        if WIDTH[m] == 256:
            return i, z
        return odd * 8 + i, lax.div(z, 2)

    def across_z(m):
        if EARLY[m]:
            wait_ring(m)
            total = jnp.concatenate([total_of(m, 0), total_of(m, 1)]).T
        else:
            wait(yrecv[m], r["yr_sem"].at[m])
            total = (own[m][y_hi] + yrecv[m][...].astype(F32)).T
        for i in range(WIDTH[m] // 16):
            for to in range(2):
                rows = total[16 * i + 8 * to : 16 * i + 8 * to + 8]
                zsend[m][i, to] = jnp.concatenate([rows[:, :128], rows[:, 128:]]).astype(BF16)

        def post(i, carry):
            to_z, slot = owner_of(m, i)

            def copy(to, sem):
                pltpu.make_async_remote_copy(
                    src_ref=zsend[m].at[i, to], dst_ref=zrecv[m].at[slot, core], send_sem=zs_sem.at[m, sem],
                    recv_sem=zr_sem.at[m, slot], device_id=device(dz=to_z - z, at=to), device_id_type=MESH,
                ).start()

            @pl.when(to_z != z)
            def _():
                copy(0, 0)
                copy(1, 0)

            @pl.when(to_z == z)
            def _():
                copy(other, 1)
                zrecv[m][slot, core] = zsend[m][i, core]

            return carry

        lax.fori_loop(0, WIDTH[m] // 16, post, 0)

    def owned(m):
        count = WIDTH[m] // 16

        def arrive(i, carry):
            from_z = i if count == NZ else 2 * i + lax.div(z, 8)

            @pl.when(from_z != z)
            def _():
                wait(zrecv[m].at[i], zr_sem.at[m, i])

            @pl.when(from_z == z)
            def _():
                wait(zrecv[m].at[i, other], zr_sem.at[m, i])

            return carry

        lax.fori_loop(0, count, arrive, 0)
        for half in range(2):
            total = zrecv[m][0, half].astype(F32)
            for i in range(1, count):
                total = total + zrecv[m][i, half].astype(F32)
            total = total * (1.0 / 256.0)
            for part in range(2):
                first = half * HK + part * 128
                wg_ref[m, :, first : first + 128] = total[8 * part : 8 * part + 8]

    def left(m):
        count = WIDTH[m] // 16
        to_self = (odd * 8 <= z) & (z < odd * 8 + 8)
        if count == NZ:
            wait(zsend[m].at[pl.ds(0, NZ - 1)], zs_sem.at[m, 0])
            wait(zsend[m].at[0, 0], zs_sem.at[m, 1])
            return

        @pl.when(to_self)
        def _():
            wait(zsend[m].at[pl.ds(0, count - 1)], zs_sem.at[m, 0])
            wait(zsend[m].at[0, 0], zs_sem.at[m, 1])

        @pl.when(jnp.logical_not(to_self))
        def _():
            wait(zsend[m], zs_sem.at[m, 0])

    def input_grad(b, carry):
        columns = aligned(b, Q)
        block, half = lax.div(b, 2), lax.rem(b, 2)
        rows = aligned(half, Q)
        total = lax.dot_general(gn[0], w[0, block, rows, :], NT, preferred_element_type=F32)
        total += lax.dot_general(gn[1], w[1, block, rows, :], NT, preferred_element_type=F32)

        @pl.when(core == 0)
        def _():
            igk[0, :, columns] = total[0:128]
            igk[1, :, columns] = total[256:384]
            igs[0, :, columns] = total[384:512].astype(BF16)
            igs[1, :, columns] = total[128:256].astype(BF16)

        @pl.when(core == 1)
        def _():
            igk[0, :, columns] = total[384:512]
            igk[1, :, columns] = total[128:256]
            igs[0, :, columns] = total[0:128].astype(BF16)
            igs[1, :, columns] = total[256:384].astype(BF16)

        return carry

    wait_partial(0)
    wait_partial(1)
    lax.fori_loop(0, 4, elementwise_hidden, 0)
    early = len(sent)
    order = (across, before, after, x)
    for block in order:
        pair(2, block)
    swap_y(2, across)
    wait_partial(2)
    lax.fori_loop(0, 4, elementwise_grads, 0)
    send_across(0)
    swap_y(2, before)
    send_near(0)
    for block in order:
        pair(1, block)
    swap_y(2, after)
    swap_y(2, x)
    lax.fori_loop(0, 4, input_grad, 0)
    send_across(2)
    swap_y(1, across)
    send_near(2)
    swap_y(1, before)
    send_far(0)
    keep(2)
    keep(0)
    swap_y(1, after)
    send_far(2)
    swap_y(1, x)
    send_across(1)
    lax.fori_loop(4, 8, input_grad, 0)
    send(igs, igr, r["is_sem"].at[0], r["ir_sem"].at[0], device(at=other))
    drain(early)
    across_y(0)
    send_near(1)
    across_z(2)
    send_far(1)
    keep(1)
    across_z(1)
    wait(igr, r["ir_sem"].at[0])
    for slot in (1, 0):
        igo[slot] = (igk[slot] + igr[slot].astype(F32)).astype(BF16)
    send(igo.at[1], ig_hbm.at[:, mine], r["is_sem"].at[1], r["ir_sem"].at[1], device(dy=-side))
    done = pltpu.make_async_copy(igo.at[0], ig_hbm.at[:, mine], local_sem.at[5])
    done.start()
    across_z(0)
    owned(2)
    left(2)
    owned(1)
    left(1)
    done.wait()
    wait(ig_hbm.at[:, theirs], r["ir_sem"].at[1])
    drain(len(sent))
    left(0)
    owned(0)


def local(tokens, grad_out, quant_weights, block_scales):
    any_space = pl.BlockSpec(memory_space=pl.ANY)
    vmem = pl.BlockSpec(memory_space=pltpu.VMEM)
    return pl.pallas_call(
        kernel,
        out_shape=(
            jax.ShapeDtypeStruct((TOK, 2 * HALF), BF16),
            jax.ShapeDtypeStruct((3, 8, 2 * HK), F32),
        ),
        in_specs=[any_space, any_space, any_space, vmem],
        out_specs=(any_space, vmem),
        scratch_shapes=list(scratch().values()),
        compiler_params=pltpu.CompilerParams(
            collective_id=0, has_side_effects=True, vmem_limit_bytes=56 * 1024 * 1024
        ),
    )(tokens, grad_out, quant_weights, block_scales)


def solution(mesh):
    return jax.shard_map(
        local,
        mesh=mesh,
        in_specs=(
            P(("inner", "outer"), None),
            P(("inner", "outer"), None),
            P(None, "inner", None, None),
            P(None, "inner", None),
        ),
        out_specs=(P(("inner", "outer"), None), P(None, ("inner", "outer"), None)),
        check_vma=False,
    )
```

```python
import jax
import jax.numpy as jnp
from jax import lax
from jax.experimental import pallas as pl
from jax.experimental.pallas import tpu as pltpu
from jax.sharding import PartitionSpec as P

MESH = pl.DeviceIdType.MESH
BF16, F32 = jnp.bfloat16, jnp.float32
NX, NY, NZ = 4, 4, 16
TOK = 128
HALF = 2048
HK = 256
Q = 256
WIDTH = (256, 128, 128)
EARLY = (False, True, True)
NT = (((1,), (1,)), ((), ()))


def scratch():
    vmem, dma = pltpu.VMEM, pltpu.SemaphoreType.DMA
    shapes = {
        "xt": vmem((4 * TOK, HALF), BF16),
        "xg": vmem((4 * TOK, HALF), BF16),
        "away": vmem((2, TOK, HALF), BF16),
        "quant": vmem((3, 4, 128, HK), BF16),
        "w": vmem((3, NX, 512, HK), BF16),
        "pacc": vmem((3, 4 * TOK, HK), F32),
        "psend": vmem((3, 4 * TOK, HK), BF16),
        "precv": vmem((3, 4 * TOK, HK), BF16),
        "gn": vmem((2, 4 * TOK, HK), BF16),
        "gt": vmem((3, HK, 4 * TOK), BF16),
        "pair_keep": vmem((3, NX, 2, HK, 128), F32),
        "pair_send": vmem((3, NX, 2, HK, 128), BF16),
        "pair_recv": vmem((3, NX, 2, HK, 128), BF16),
        "early_send": vmem((3, NX, HK, 128), BF16),
        "early_recv": vmem((3, NX, HK, 128), BF16),
        "igk": vmem((2, TOK, HALF), F32),
        "igs": vmem((2, TOK, HALF), BF16),
        "igr": vmem((2, TOK, HALF), BF16),
        "igo": vmem((2, TOK, HALF), BF16),
        "local_sem": dma((6,)),
        "xs_sem": dma((2, 5)), "xr_sem": dma((2, 5)),
        "ws_sem": dma((3, 10)), "wr_sem": dma((3, 10)),
        "ps_sem": dma((3, 2)), "pr_sem": dma((3, 2)),
        "cs_sem": dma((3, NX, 2)), "cr_sem": dma((3, NX, 2)),
        "rs_sem": dma((3, 6)), "rr_sem": dma((3, 6)),
        "es_sem": dma((3, NX)), "er_sem": dma((3, NX)),
        "ys_sem": dma((3,)), "yr_sem": dma((3,)),
        "zs_sem": dma((3, 2)), "zr_sem": dma((3, NZ)),
        "is_sem": dma((2,)), "ir_sem": dma((2,)),
    }
    for m, width in enumerate(WIDTH):
        piece = (128 if EARLY[m] else 256, width)
        shapes |= {
            f"dws{m}": vmem((6, *piece), BF16),
            f"own{m}": vmem((2, *piece), F32),
            f"relay{m}": vmem((2, *piece), BF16),
            f"near{m}": vmem((2, *piece), BF16),
            f"far{m}": vmem((2, *piece), BF16),
            f"ysend{m}": vmem(piece, BF16),
            f"yrecv{m}": vmem(piece, BF16),
            f"zsend{m}": vmem((width // 16, 2, 16, 128), BF16),
            f"zrecv{m}": vmem((width // 16, 2, 16, 128), BF16),
        }
    return shapes


def aligned(index, size):
    return pl.ds(pl.multiple_of(index * size, size), size)


def dot(a, b):
    return jnp.dot(a, b, preferred_element_type=F32)


def kernel(tok_hbm, out_hbm, quant_hbm, scales, ig_hbm, wg_ref, *scratch_refs):
    r = dict(zip(scratch(), scratch_refs, strict=True))
    xt, xg, away, quant, w, pacc, psend, precv, gn, gt = (
        r[name] for name in ("xt", "xg", "away", "quant", "w", "pacc", "psend", "precv", "gn", "gt")
    )
    pair_keep, pair_send, pair_recv = r["pair_keep"], r["pair_send"], r["pair_recv"]
    igk, igs, igr, igo = (r[name] for name in ("igk", "igs", "igr", "igo"))
    local_sem, xs_sem, xr_sem, ws_sem, wr_sem = (
        r[name] for name in ("local_sem", "xs_sem", "xr_sem", "ws_sem", "wr_sem")
    )
    dws, own, relay, near, far, ysend, yrecv, zsend, zrecv = (
        [r[f"{name}{m}"] for m in range(3)]
        for name in ("dws", "own", "relay", "near", "far", "ysend", "yrecv", "zsend", "zrecv")
    )
    early_send, early_recv = r["early_send"], r["early_recv"]

    inner, outer = lax.axis_index("inner"), lax.axis_index("outer")
    x, y_lo = lax.rem(inner, NX), lax.div(inner, NX)
    core, z = lax.rem(outer, 2), lax.rem(lax.div(outer, 2), NZ)
    y_hi = lax.div(outer, 2 * NZ)
    y = 2 * y_hi + y_lo
    other = 1 - core
    odd = lax.rem(z, 2)
    before, after, across = (lax.rem(x + step, NX) for step in (3, 1, 2))

    def device(dx=0, dy=0, dz=0, at=core):
        to_x, to_y, to_z = (
            lax.rem(x + dx + NX, NX),
            lax.rem(y + dy + NY, NY),
            lax.rem(z + dz + NZ, NZ),
        )
        return (
            lax.rem(to_y, 2) * NX + to_x,
            (lax.div(to_y, 2) * NZ + to_z) * 2 + at,
        )

    sent = []

    def drain(count):
        for src, sem in sent[:count]:
            wait(src, sem)
        del sent[:count]

    def send(src, dst, s_sem, r_sem, to):
        pltpu.make_async_remote_copy(
            src_ref=src, dst_ref=dst, send_sem=s_sem, recv_sem=r_sem, device_id=to, device_id_type=MESH
        ).start()
        sent.append((src, s_sem))

    def wait(ref, sem):
        pltpu.make_async_copy(ref, ref, sem).wait()

    side = 1 - 2 * core
    mine, theirs = aligned(y_lo, HALF), aligned(1 - y_lo, HALF)
    hidden_half = aligned(core, HK)

    own_rows = aligned(3 * core, TOK)
    pltpu.make_async_copy(quant_hbm.at[:, :, :, hidden_half], quant, local_sem.at[0]).start()
    pltpu.make_async_copy(tok_hbm.at[:, mine], xt.at[own_rows, :], local_sem.at[1]).start()
    pltpu.make_async_copy(out_hbm.at[:, mine], xg.at[own_rows, :], local_sem.at[2]).start()
    pltpu.make_async_copy(tok_hbm.at[:, theirs], away.at[0], local_sem.at[3]).start()
    pltpu.make_async_copy(out_hbm.at[:, theirs], away.at[1], local_sem.at[4]).start()

    barrier = pltpu.get_barrier_semaphore()
    partners = [
        device(at=other), device(dx=1), device(dx=-1), device(dy=1), device(dy=-1), device(dy=2),
        device(dy=side, at=other),
    ]
    column = outer - 2 * z - core
    for j in sorted(range(1, NZ), key=lambda j: -min(j, NZ - j)):
        for at in range(2):
            to = column + 2 * ((z + j) & (NZ - 1)) + at
            pl.semaphore_signal(barrier, inc=1, device_id=(inner, to), device_id_type=MESH)
    for to in partners:
        pl.semaphore_signal(barrier, inc=1, device_id=to, device_id_type=MESH)

    def dequantise(m):
        for b in range(4):
            scale = scales[m, pl.ds(b, 1), hidden_half]
            w[m, x, b * 128 : (b + 1) * 128, :] = (quant[m, b].astype(F32) * scale).astype(BF16)

    wait(quant, local_sem.at[0])
    dequantise(0)
    pl.semaphore_wait(barrier, len(partners) + 2 * (NZ - 1))

    def send_tokens(a, dst):
        wait(away.at[a], local_sem.at[3 + a])
        for part in range(2):
            rows = pl.ds(part * 64, 64)
            to_rows = pl.ds(pl.multiple_of((2 - core) * TOK + part * 64, 64), 64)
            send(
                away.at[a, rows, :], dst.at[to_rows, :], xs_sem.at[a, part], xr_sem.at[a, core],
                device(dy=side, at=part),
            )
        wait(dst.at[own_rows, :], local_sem.at[1 + a])
        send(dst.at[own_rows, :], dst.at[own_rows, :], xs_sem.at[a, 2], xr_sem.at[a, 2], device(at=other))

    def pass_tokens(a, dst):
        for i, block in enumerate((2, 1)):
            rows = pl.ds(pl.multiple_of(block * TOK + core * 64, 64), 64)
            wait(dst.at[rows, :], xr_sem.at[a, i])
            send(dst.at[rows, :], dst.at[rows, :], xs_sem.at[a, 3 + i], xr_sem.at[a, 3 + i], device(at=other))

    def wait_tokens(a, dst):
        wait(dst.at[aligned(3 - 3 * core, TOK), :], xr_sem.at[a, 2])
        for i, block in enumerate((2, 1)):
            rows = pl.ds(pl.multiple_of(block * TOK + other * 64, 64), 64)
            wait(dst.at[rows, :], xr_sem.at[a, 3 + i])

    def quarter(m, shard, half, q):
        return w.at[m, shard, pl.ds(pl.multiple_of(half * 256 + q * 128, 128), 128), :]

    def half_of(m, shard):
        return w.at[m, shard, aligned(odd, 256), :]

    def pass_on(m, ref, channel, to):
        send(ref, ref, ws_sem.at[m, channel], wr_sem.at[m, channel], to)

    def send_weights(m):
        pass_on(m, half_of(m, x), 0, device(dx=1))
        pass_on(m, half_of(m, x), 1, device(dx=-1))

    def relay_weights(m):
        for i, (shard, step) in enumerate(((before, 1), (after, -1))):
            wait(half_of(m, shard), wr_sem.at[m, i])
            pass_on(m, quarter(m, shard, odd, i), 2 + i, device(dx=step))
            pass_on(m, quarter(m, shard, odd, 0), 4 + 2 * i, device(dz=1))
            pass_on(m, quarter(m, shard, odd, 1), 5 + 2 * i, device(dz=-1))

    def relay_across(m):
        for q, step in ((0, 1), (1, -1)):
            wait(quarter(m, across, odd, q), wr_sem.at[m, 2 + q])
            pass_on(m, quarter(m, across, odd, q), 8 + q, device(dz=step))

    def term(m, shard, half):
        columns = aligned(shard * 2 + half, 256)
        return dot((xg if m == 2 else xt)[:, columns], w[m, shard, aligned(half, 256), :])

    def first_terms(m):
        pacc[m] = term(m, x, 0) + term(m, x, 1) + term(m, before, odd) + term(m, after, odd)

    def last_terms(m):
        for i, shard in enumerate((before, after, across)):
            for q in range(2):
                wait(quarter(m, shard, 1 - odd, q), wr_sem.at[m, 4 + 2 * i + q])
        total = (
            pacc[m] + term(m, before, 1 - odd) + term(m, after, 1 - odd)
            + term(m, across, 0) + term(m, across, 1)
        )
        pacc[m] = total
        psend[m] = total.astype(BF16)
        low, high = pl.ds(0, 256), pl.ds(256, 256)
        send(psend.at[m, low], precv.at[m, high], r["ps_sem"].at[m, 0], r["pr_sem"].at[m, 0], device(dy=1))
        send(psend.at[m, high], precv.at[m, low], r["ps_sem"].at[m, 1], r["pr_sem"].at[m, 1], device(dy=-1))

    send_weights(0)
    send_tokens(0, xt)
    dequantise(1)
    send_weights(1)
    dequantise(2)
    relay_weights(0)
    send_tokens(1, xg)
    relay_weights(1)
    send_weights(2)
    relay_across(0)
    pass_tokens(0, xt)
    relay_across(1)
    wait_tokens(0, xt)
    first_terms(0)
    relay_weights(2)
    last_terms(0)
    first_terms(1)
    last_terms(1)
    relay_across(2)
    pass_tokens(1, xg)
    wait_tokens(1, xg)
    first_terms(2)
    last_terms(2)

    def wait_partial(m):
        wait(precv.at[m, pl.ds(256, 256)], r["pr_sem"].at[m, 0])
        wait(precv.at[m, pl.ds(0, 256)], r["pr_sem"].at[m, 1])

    def elementwise_hidden(b, carry):
        rows = aligned(b, 128)
        gate, up = (pacc[m, rows, :] + precv[m, rows, :].astype(F32) for m in range(2))
        s = jax.nn.sigmoid(gate)
        pacc[0, rows, :] = gate * s
        pacc[1, rows, :] = up * s * (1.0 + gate * (1.0 - s))
        gt[2, :, rows] = (gate * s * up).astype(BF16).T
        return carry

    def elementwise_grads(b, carry):
        rows = aligned(b, 128)
        d_hidden = pacc[2, rows, :] + precv[2, rows, :].astype(F32)
        grad_up = (d_hidden * pacc[0, rows, :]).astype(BF16)
        grad_gate = (d_hidden * pacc[1, rows, :]).astype(BF16)
        gn[0, rows, :] = grad_gate
        gn[1, rows, :] = grad_up
        gt[0, :, rows] = grad_gate.T
        gt[1, :, rows] = grad_up.T
        return carry

    def product(m, block, half):
        return dot(gt[m], (xg if m == 2 else xt)[:, aligned(block * 2 + half, Q)])

    def pair(m, block):
        for half in range(2):
            value = product(m, block, half)
            low, high = value[:, :128], value[:, 128:]
            pair_keep[m, block, half] = jnp.where(odd == 0, low, high)
            pair_send[m, block, half] = jnp.where(odd == 0, high, low).astype(BF16)
        for part, step in ((0, 1), (1, -1)):
            rows = pl.ds(part * 128, 128)
            send(
                pair_send.at[m, block, :, rows, :], pair_recv.at[m, block, :, rows, :],
                r["cs_sem"].at[m, block, part], r["cr_sem"].at[m, block, part], device(dz=step),
            )

    def wait_pair(m, block):
        for part in range(2):
            rows = pl.ds(part * 128, 128)
            wait(pair_recv.at[m, block, :, rows, :], r["cr_sem"].at[m, block, part])

    def swap_y(m, block):
        wait_pair(m, block)
        gone = 1 - y_hi
        early_send[m, block] = (
            pair_keep[m, block, gone] + pair_recv[m, block, gone].astype(F32)
        ).astype(BF16)
        send(
            early_send.at[m, block], early_recv.at[m, block], r["es_sem"].at[m, block], r["er_sem"].at[m, block],
            device(dy=2),
        )

    def wait_block(m, block):
        if EARLY[m]:
            wait(early_recv.at[m, block], r["er_sem"].at[m, block])
        elif WIDTH[m] == 128:
            wait_pair(m, block)

    def value_of(m, block, half):
        if EARLY[m]:
            rows = pl.ds(half * 128, 128)
            return (
                pair_keep[m, block, y_hi, rows, :]
                + pair_recv[m, block, y_hi, rows, :].astype(F32)
                + early_recv[m, block, rows, :].astype(F32)
            )
        if WIDTH[m] == 128:
            return pair_keep[m, block, half] + pair_recv[m, block, half].astype(F32)
        return product(m, block, half)

    def ring_send(m, slot, value, dst, step):
        dws[m][slot] = value.astype(BF16)
        send(dws[m].at[slot], dst, r["rs_sem"].at[m, slot], r["rr_sem"].at[m, slot], device(dx=step))

    def send_across(m):
        wait_block(m, across)
        for half, step in ((0, 1), (1, -1)):
            ring_send(m, half, value_of(m, across, half), relay[m].at[half], step)

    def send_near(m):
        wait_block(m, before)
        wait_block(m, after)
        for half, step, block in ((0, -1, before), (1, 1, after)):
            ring_send(m, 2 + half, value_of(m, block, half), near[m].at[half], step)

    def send_far(m):
        for half, step, block in ((0, 1, after), (1, -1, before)):
            value = value_of(m, block, half)
            wait(relay[m].at[half], r["rr_sem"].at[m, half])
            ring_send(m, 4 + half, value + relay[m][half].astype(F32), far[m].at[half], step)

    def keep(m):
        wait_block(m, x)
        for half in range(2):
            own[m][half] = value_of(m, x, half)

    def total_of(m, half):
        return own[m][half] + near[m][half].astype(F32) + far[m][half].astype(F32)

    def wait_ring(m):
        for half in range(2):
            wait(near[m].at[half], r["rr_sem"].at[m, 2 + half])
            wait(far[m].at[half], r["rr_sem"].at[m, 4 + half])

    def across_y(m):
        wait_ring(m)
        ysend[m][...] = total_of(m, 1 - y_hi).astype(BF16)
        send(ysend[m], yrecv[m], r["ys_sem"].at[m], r["yr_sem"].at[m], device(dy=2))
        own[m][y_hi] = total_of(m, y_hi)

    zs_sem, zr_sem = r["zs_sem"], r["zr_sem"]

    def owner_of(m, i):
        if WIDTH[m] == 256:
            return i, z
        return odd * 8 + i, lax.div(z, 2)

    def across_z(m):
        if EARLY[m]:
            wait_ring(m)
            total = jnp.concatenate([total_of(m, 0), total_of(m, 1)]).T
        else:
            wait(yrecv[m], r["yr_sem"].at[m])
            total = (own[m][y_hi] + yrecv[m][...].astype(F32)).T
        for i in range(WIDTH[m] // 16):
            for to in range(2):
                rows = total[16 * i + 8 * to : 16 * i + 8 * to + 8]
                zsend[m][i, to] = jnp.concatenate([rows[:, :128], rows[:, 128:]]).astype(BF16)

        def post(i, carry):
            to_z, slot = owner_of(m, i)

            def copy(to, sem):
                pltpu.make_async_remote_copy(
                    src_ref=zsend[m].at[i, to], dst_ref=zrecv[m].at[slot, core], send_sem=zs_sem.at[m, sem],
                    recv_sem=zr_sem.at[m, slot], device_id=device(dz=to_z - z, at=to), device_id_type=MESH,
                ).start()

            @pl.when(to_z != z)
            def _():
                copy(0, 0)
                copy(1, 0)

            @pl.when(to_z == z)
            def _():
                copy(other, 1)
                zrecv[m][slot, core] = zsend[m][i, core]

            return carry

        lax.fori_loop(0, WIDTH[m] // 16, post, 0)

    def owned(m):
        count = WIDTH[m] // 16

        def arrive(i, carry):
            from_z = i if count == NZ else 2 * i + lax.div(z, 8)

            @pl.when(from_z != z)
            def _():
                wait(zrecv[m].at[i], zr_sem.at[m, i])

            @pl.when(from_z == z)
            def _():
                wait(zrecv[m].at[i, other], zr_sem.at[m, i])

            return carry

        lax.fori_loop(0, count, arrive, 0)
        for half in range(2):
            total = zrecv[m][0, half].astype(F32)
            for i in range(1, count):
                total = total + zrecv[m][i, half].astype(F32)
            total = total * (1.0 / 256.0)
            for part in range(2):
                first = half * HK + part * 128
                wg_ref[m, :, first : first + 128] = total[8 * part : 8 * part + 8]

    def left(m):
        count = WIDTH[m] // 16
        to_self = (odd * 8 <= z) & (z < odd * 8 + 8)
        if count == NZ:
            wait(zsend[m].at[pl.ds(0, NZ - 1)], zs_sem.at[m, 0])
            wait(zsend[m].at[0, 0], zs_sem.at[m, 1])
            return

        @pl.when(to_self)
        def _():
            wait(zsend[m].at[pl.ds(0, count - 1)], zs_sem.at[m, 0])
            wait(zsend[m].at[0, 0], zs_sem.at[m, 1])

        @pl.when(jnp.logical_not(to_self))
        def _():
            wait(zsend[m], zs_sem.at[m, 0])

    def input_grad(b, carry):
        columns = aligned(b, Q)
        block, half = lax.div(b, 2), lax.rem(b, 2)
        rows = aligned(half, Q)
        total = lax.dot_general(gn[0], w[0, block, rows, :], NT, preferred_element_type=F32)
        total += lax.dot_general(gn[1], w[1, block, rows, :], NT, preferred_element_type=F32)

        @pl.when(core == 0)
        def _():
            igk[0, :, columns] = total[0:128]
            igk[1, :, columns] = total[256:384]
            igs[0, :, columns] = total[384:512].astype(BF16)
            igs[1, :, columns] = total[128:256].astype(BF16)

        @pl.when(core == 1)
        def _():
            igk[0, :, columns] = total[384:512]
            igk[1, :, columns] = total[128:256]
            igs[0, :, columns] = total[0:128].astype(BF16)
            igs[1, :, columns] = total[256:384].astype(BF16)

        return carry

    wait_partial(0)
    wait_partial(1)
    lax.fori_loop(0, 4, elementwise_hidden, 0)
    early = len(sent)
    order = (across, before, after, x)
    for block in order:
        pair(2, block)
    swap_y(2, across)
    wait_partial(2)
    lax.fori_loop(0, 4, elementwise_grads, 0)
    send_across(0)
    swap_y(2, before)
    send_near(0)
    for block in order:
        pair(1, block)
    swap_y(2, after)
    swap_y(2, x)
    lax.fori_loop(0, 4, input_grad, 0)
    send_across(2)
    swap_y(1, across)
    send_near(2)
    swap_y(1, before)
    send_far(0)
    keep(2)
    keep(0)
    swap_y(1, after)
    send_far(2)
    swap_y(1, x)
    send_across(1)
    lax.fori_loop(4, 8, input_grad, 0)
    send(igs, igr, r["is_sem"].at[0], r["ir_sem"].at[0], device(at=other))
    drain(early)
    across_y(0)
    send_near(1)
    across_z(2)
    send_far(1)
    keep(1)
    across_z(1)
    wait(igr, r["ir_sem"].at[0])
    for slot in (1, 0):
        igo[slot] = (igk[slot] + igr[slot].astype(F32)).astype(BF16)
    send(igo.at[1], ig_hbm.at[:, mine], r["is_sem"].at[1], r["ir_sem"].at[1], device(dy=-side))
    done = pltpu.make_async_copy(igo.at[0], ig_hbm.at[:, mine], local_sem.at[5])
    done.start()
    across_z(0)
    owned(2)
    left(2)
    owned(1)
    left(1)
    done.wait()
    wait(ig_hbm.at[:, theirs], r["ir_sem"].at[1])
    drain(len(sent))
    left(0)
    owned(0)


def local(tokens, grad_out, quant_weights, block_scales):
    any_space = pl.BlockSpec(memory_space=pl.ANY)
    vmem = pl.BlockSpec(memory_space=pltpu.VMEM)
    return pl.pallas_call(
        kernel,
        out_shape=(
            jax.ShapeDtypeStruct((TOK, 2 * HALF), BF16),
            jax.ShapeDtypeStruct((3, 8, 2 * HK), F32),
        ),
        in_specs=[any_space, any_space, any_space, vmem],
        out_specs=(any_space, vmem),
        scratch_shapes=list(scratch().values()),
        compiler_params=pltpu.CompilerParams(
            collective_id=0, has_side_effects=True, vmem_limit_bytes=56 * 1024 * 1024
        ),
    )(tokens, grad_out, quant_weights, block_scales)


def solution(mesh):
    return jax.shard_map(
        local,
        mesh=mesh,
        in_specs=(
            P(("inner", "outer"), None),
            P(("inner", "outer"), None),
            P(None, "inner", None, None),
            P(None, "inner", None),
        ),
        out_specs=(P(("inner", "outer"), None), P(None, ("inner", "outer"), None)),
        check_vma=False,
    )
```

```python
import jax
import jax.numpy as jnp
from jax import lax
from jax.experimental import pallas as pl
from jax.experimental.pallas import tpu as pltpu
from jax.sharding import PartitionSpec as P

MESH = pl.DeviceIdType.MESH
BF16, F32 = jnp.bfloat16, jnp.float32
NX, NY, NZ = 4, 4, 16
TOK = 128
HALF = 2048
HK = 256
Q = 256
WIDTH = (256, 128, 128)
EARLY = (False, True, True)
NT = (((1,), (1,)), ((), ()))


def scratch():
    vmem, dma = pltpu.VMEM, pltpu.SemaphoreType.DMA
    shapes = {
        "xt": vmem((4 * TOK, HALF), BF16),
        "xg": vmem((4 * TOK, HALF), BF16),
        "away": vmem((2, TOK, HALF), BF16),
        "quant": vmem((3, 4, 128, HK), BF16),
        "w": vmem((3, NX, 512, HK), BF16),
        "pacc": vmem((3, 4 * TOK, HK), F32),
        "psend": vmem((3, 4 * TOK, HK), BF16),
        "precv": vmem((3, 4 * TOK, HK), BF16),
        "gn": vmem((2, 4 * TOK, HK), BF16),
        "gt": vmem((3, HK, 4 * TOK), BF16),
        "pair_keep": vmem((3, NX, 2, HK, 128), F32),
        "pair_send": vmem((3, NX, 2, HK, 128), BF16),
        "pair_recv": vmem((3, NX, 2, HK, 128), BF16),
        "early_send": vmem((3, NX, HK, 128), BF16),
        "early_recv": vmem((3, NX, HK, 128), BF16),
        "igk": vmem((2, TOK, HALF), F32),
        "igs": vmem((2, TOK, HALF), BF16),
        "igr": vmem((2, TOK, HALF), BF16),
        "igo": vmem((2, TOK, HALF), BF16),
        "local_sem": dma((6,)),
        "xs_sem": dma((2, 5)), "xr_sem": dma((2, 5)),
        "ws_sem": dma((3, 10)), "wr_sem": dma((3, 10)),
        "ps_sem": dma((3, 2)), "pr_sem": dma((3, 2)),
        "cs_sem": dma((3, NX, 2)), "cr_sem": dma((3, NX, 2)),
        "rs_sem": dma((3, 6)), "rr_sem": dma((3, 6)),
        "es_sem": dma((3, NX)), "er_sem": dma((3, NX)),
        "ys_sem": dma((3,)), "yr_sem": dma((3,)),
        "zs_sem": dma((3, 2)), "zr_sem": dma((3, NZ)),
        "is_sem": dma((2,)), "ir_sem": dma((2,)),
    }
    for m, width in enumerate(WIDTH):
        piece = (128 if EARLY[m] else 256, width)
        shapes |= {
            f"dws{m}": vmem((6, *piece), BF16),
            f"own{m}": vmem((2, *piece), F32),
            f"relay{m}": vmem((2, *piece), BF16),
            f"near{m}": vmem((2, *piece), BF16),
            f"far{m}": vmem((2, *piece), BF16),
            f"ysend{m}": vmem(piece, BF16),
            f"yrecv{m}": vmem(piece, BF16),
            f"zsend{m}": vmem((width // 16, 2, 16, 128), BF16),
            f"zrecv{m}": vmem((width // 16, 2, 16, 128), BF16),
        }
    return shapes


def aligned(index, size):
    return pl.ds(pl.multiple_of(index * size, size), size)


def dot(a, b):
    return jnp.dot(a, b, preferred_element_type=F32)


def kernel(tok_hbm, out_hbm, quant_hbm, scales, ig_hbm, wg_ref, *scratch_refs):
    r = dict(zip(scratch(), scratch_refs, strict=True))
    xt, xg, away, quant, w, pacc, psend, precv, gn, gt = (
        r[name] for name in ("xt", "xg", "away", "quant", "w", "pacc", "psend", "precv", "gn", "gt")
    )
    pair_keep, pair_send, pair_recv = r["pair_keep"], r["pair_send"], r["pair_recv"]
    igk, igs, igr, igo = (r[name] for name in ("igk", "igs", "igr", "igo"))
    local_sem, xs_sem, xr_sem, ws_sem, wr_sem = (
        r[name] for name in ("local_sem", "xs_sem", "xr_sem", "ws_sem", "wr_sem")
    )
    dws, own, relay, near, far, ysend, yrecv, zsend, zrecv = (
        [r[f"{name}{m}"] for m in range(3)]
        for name in ("dws", "own", "relay", "near", "far", "ysend", "yrecv", "zsend", "zrecv")
    )
    early_send, early_recv = r["early_send"], r["early_recv"]

    inner, outer = lax.axis_index("inner"), lax.axis_index("outer")
    x, y_lo = lax.rem(inner, NX), lax.div(inner, NX)
    core, z = lax.rem(outer, 2), lax.rem(lax.div(outer, 2), NZ)
    y_hi = lax.div(outer, 2 * NZ)
    y = 2 * y_hi + y_lo
    other = 1 - core
    odd = lax.rem(z, 2)
    before, after, across = (lax.rem(x + step, NX) for step in (3, 1, 2))

    def device(dx=0, dy=0, dz=0, at=core):
        to_x, to_y, to_z = (
            lax.rem(x + dx + NX, NX),
            lax.rem(y + dy + NY, NY),
            lax.rem(z + dz + NZ, NZ),
        )
        return (
            lax.rem(to_y, 2) * NX + to_x,
            (lax.div(to_y, 2) * NZ + to_z) * 2 + at,
        )

    sent = []

    def drain(count):
        for src, sem in sent[:count]:
            wait(src, sem)
        del sent[:count]

    def send(src, dst, s_sem, r_sem, to):
        pltpu.make_async_remote_copy(
            src_ref=src, dst_ref=dst, send_sem=s_sem, recv_sem=r_sem, device_id=to, device_id_type=MESH
        ).start()
        sent.append((src, s_sem))

    def wait(ref, sem):
        pltpu.make_async_copy(ref, ref, sem).wait()

    side = 1 - 2 * core
    mine, theirs = aligned(y_lo, HALF), aligned(1 - y_lo, HALF)
    hidden_half = aligned(core, HK)

    own_rows = aligned(3 * core, TOK)
    pltpu.make_async_copy(quant_hbm.at[:, :, :, hidden_half], quant, local_sem.at[0]).start()
    pltpu.make_async_copy(tok_hbm.at[:, mine], xt.at[own_rows, :], local_sem.at[1]).start()
    pltpu.make_async_copy(out_hbm.at[:, mine], xg.at[own_rows, :], local_sem.at[2]).start()
    pltpu.make_async_copy(tok_hbm.at[:, theirs], away.at[0], local_sem.at[3]).start()
    pltpu.make_async_copy(out_hbm.at[:, theirs], away.at[1], local_sem.at[4]).start()

    barrier = pltpu.get_barrier_semaphore()
    partners = [
        device(at=other), device(dx=1), device(dx=-1), device(dy=1), device(dy=-1), device(dy=2),
        device(dy=side, at=other),
    ]
    column = outer - 2 * z - core
    for j in sorted(range(1, NZ), key=lambda j: -min(j, NZ - j)):
        for at in range(2):
            to = column + 2 * ((z + j) & (NZ - 1)) + at
            pl.semaphore_signal(barrier, inc=1, device_id=(inner, to), device_id_type=MESH)
    for to in partners:
        pl.semaphore_signal(barrier, inc=1, device_id=to, device_id_type=MESH)

    def dequantise(m):
        for b in range(4):
            scale = scales[m, pl.ds(b, 1), hidden_half]
            w[m, x, b * 128 : (b + 1) * 128, :] = (quant[m, b].astype(F32) * scale).astype(BF16)

    wait(quant, local_sem.at[0])
    dequantise(0)
    pl.semaphore_wait(barrier, len(partners) + 2 * (NZ - 1))

    def send_tokens(a, dst):
        wait(away.at[a], local_sem.at[3 + a])
        for part in range(2):
            rows = pl.ds(part * 64, 64)
            to_rows = pl.ds(pl.multiple_of((2 - core) * TOK + part * 64, 64), 64)
            send(
                away.at[a, rows, :], dst.at[to_rows, :], xs_sem.at[a, part], xr_sem.at[a, core],
                device(dy=side, at=part),
            )
        wait(dst.at[own_rows, :], local_sem.at[1 + a])
        send(dst.at[own_rows, :], dst.at[own_rows, :], xs_sem.at[a, 2], xr_sem.at[a, 2], device(at=other))

    def pass_tokens(a, dst):
        for i, block in enumerate((2, 1)):
            rows = pl.ds(pl.multiple_of(block * TOK + core * 64, 64), 64)
            wait(dst.at[rows, :], xr_sem.at[a, i])
            send(dst.at[rows, :], dst.at[rows, :], xs_sem.at[a, 3 + i], xr_sem.at[a, 3 + i], device(at=other))

    def wait_tokens(a, dst):
        wait(dst.at[aligned(3 - 3 * core, TOK), :], xr_sem.at[a, 2])
        for i, block in enumerate((2, 1)):
            rows = pl.ds(pl.multiple_of(block * TOK + other * 64, 64), 64)
            wait(dst.at[rows, :], xr_sem.at[a, 3 + i])

    def quarter(m, shard, half, q):
        return w.at[m, shard, pl.ds(pl.multiple_of(half * 256 + q * 128, 128), 128), :]

    def half_of(m, shard):
        return w.at[m, shard, aligned(odd, 256), :]

    def pass_on(m, ref, channel, to):
        send(ref, ref, ws_sem.at[m, channel], wr_sem.at[m, channel], to)

    def send_weights(m):
        pass_on(m, half_of(m, x), 0, device(dx=1))
        pass_on(m, half_of(m, x), 1, device(dx=-1))

    def relay_weights(m):
        for i, (shard, step) in enumerate(((before, 1), (after, -1))):
            wait(half_of(m, shard), wr_sem.at[m, i])
            pass_on(m, quarter(m, shard, odd, i), 2 + i, device(dx=step))
            pass_on(m, quarter(m, shard, odd, 0), 4 + 2 * i, device(dz=1))
            pass_on(m, quarter(m, shard, odd, 1), 5 + 2 * i, device(dz=-1))

    def relay_across(m):
        for q, step in ((0, 1), (1, -1)):
            wait(quarter(m, across, odd, q), wr_sem.at[m, 2 + q])
            pass_on(m, quarter(m, across, odd, q), 8 + q, device(dz=step))

    def term(m, shard, half):
        columns = aligned(shard * 2 + half, 256)
        return dot((xg if m == 2 else xt)[:, columns], w[m, shard, aligned(half, 256), :])

    def first_terms(m):
        pacc[m] = term(m, x, 0) + term(m, x, 1) + term(m, before, odd) + term(m, after, odd)

    def last_terms(m):
        for i, shard in enumerate((before, after, across)):
            for q in range(2):
                wait(quarter(m, shard, 1 - odd, q), wr_sem.at[m, 4 + 2 * i + q])
        total = (
            pacc[m] + term(m, before, 1 - odd) + term(m, after, 1 - odd)
            + term(m, across, 0) + term(m, across, 1)
        )
        pacc[m] = total
        psend[m] = total.astype(BF16)
        low, high = pl.ds(0, 256), pl.ds(256, 256)
        send(psend.at[m, low], precv.at[m, high], r["ps_sem"].at[m, 0], r["pr_sem"].at[m, 0], device(dy=1))
        send(psend.at[m, high], precv.at[m, low], r["ps_sem"].at[m, 1], r["pr_sem"].at[m, 1], device(dy=-1))

    send_weights(0)
    send_tokens(0, xt)
    dequantise(1)
    send_weights(1)
    dequantise(2)
    relay_weights(0)
    send_tokens(1, xg)
    relay_weights(1)
    send_weights(2)
    relay_across(0)
    pass_tokens(0, xt)
    relay_across(1)
    wait_tokens(0, xt)
    first_terms(0)
    relay_weights(2)
    last_terms(0)
    first_terms(1)
    last_terms(1)
    relay_across(2)
    pass_tokens(1, xg)
    wait_tokens(1, xg)
    first_terms(2)
    last_terms(2)

    def wait_partial(m):
        wait(precv.at[m, pl.ds(256, 256)], r["pr_sem"].at[m, 0])
        wait(precv.at[m, pl.ds(0, 256)], r["pr_sem"].at[m, 1])

    def elementwise_hidden(b, carry):
        rows = aligned(b, 128)
        gate, up = (pacc[m, rows, :] + precv[m, rows, :].astype(F32) for m in range(2))
        s = jax.nn.sigmoid(gate)
        pacc[0, rows, :] = gate * s
        pacc[1, rows, :] = up * s * (1.0 + gate * (1.0 - s))
        gt[2, :, rows] = (gate * s * up).astype(BF16).T
        return carry

    def elementwise_grads(b, carry):
        rows = aligned(b, 128)
        d_hidden = pacc[2, rows, :] + precv[2, rows, :].astype(F32)
        grad_up = (d_hidden * pacc[0, rows, :]).astype(BF16)
        grad_gate = (d_hidden * pacc[1, rows, :]).astype(BF16)
        gn[0, rows, :] = grad_gate
        gn[1, rows, :] = grad_up
        gt[0, :, rows] = grad_gate.T
        gt[1, :, rows] = grad_up.T
        return carry

    def product(m, block, half):
        return dot(gt[m], (xg if m == 2 else xt)[:, aligned(block * 2 + half, Q)])

    def pair(m, block):
        for half in range(2):
            value = product(m, block, half)
            low, high = value[:, :128], value[:, 128:]
            pair_keep[m, block, half] = jnp.where(odd == 0, low, high)
            pair_send[m, block, half] = jnp.where(odd == 0, high, low).astype(BF16)
        for part, step in ((0, 1), (1, -1)):
            rows = pl.ds(part * 128, 128)
            send(
                pair_send.at[m, block, :, rows, :], pair_recv.at[m, block, :, rows, :],
                r["cs_sem"].at[m, block, part], r["cr_sem"].at[m, block, part], device(dz=step),
            )

    def wait_pair(m, block):
        for part in range(2):
            rows = pl.ds(part * 128, 128)
            wait(pair_recv.at[m, block, :, rows, :], r["cr_sem"].at[m, block, part])

    def swap_y(m, block):
        wait_pair(m, block)
        gone = 1 - y_hi
        early_send[m, block] = (
            pair_keep[m, block, gone] + pair_recv[m, block, gone].astype(F32)
        ).astype(BF16)
        send(
            early_send.at[m, block], early_recv.at[m, block], r["es_sem"].at[m, block], r["er_sem"].at[m, block],
            device(dy=2),
        )

    def wait_block(m, block):
        if EARLY[m]:
            wait(early_recv.at[m, block], r["er_sem"].at[m, block])
        elif WIDTH[m] == 128:
            wait_pair(m, block)

    def value_of(m, block, half):
        if EARLY[m]:
            rows = pl.ds(half * 128, 128)
            return (
                pair_keep[m, block, y_hi, rows, :]
                + pair_recv[m, block, y_hi, rows, :].astype(F32)
                + early_recv[m, block, rows, :].astype(F32)
            )
        if WIDTH[m] == 128:
            return pair_keep[m, block, half] + pair_recv[m, block, half].astype(F32)
        return product(m, block, half)

    def ring_send(m, slot, value, dst, step):
        dws[m][slot] = value.astype(BF16)
        send(dws[m].at[slot], dst, r["rs_sem"].at[m, slot], r["rr_sem"].at[m, slot], device(dx=step))

    def send_across(m):
        wait_block(m, across)
        for half, step in ((0, 1), (1, -1)):
            ring_send(m, half, value_of(m, across, half), relay[m].at[half], step)

    def send_near(m):
        wait_block(m, before)
        wait_block(m, after)
        for half, step, block in ((0, -1, before), (1, 1, after)):
            ring_send(m, 2 + half, value_of(m, block, half), near[m].at[half], step)

    def send_far(m):
        for half, step, block in ((0, 1, after), (1, -1, before)):
            value = value_of(m, block, half)
            wait(relay[m].at[half], r["rr_sem"].at[m, half])
            ring_send(m, 4 + half, value + relay[m][half].astype(F32), far[m].at[half], step)

    def keep(m):
        wait_block(m, x)
        for half in range(2):
            own[m][half] = value_of(m, x, half)

    def total_of(m, half):
        return own[m][half] + near[m][half].astype(F32) + far[m][half].astype(F32)

    def wait_ring(m):
        for half in range(2):
            wait(near[m].at[half], r["rr_sem"].at[m, 2 + half])
            wait(far[m].at[half], r["rr_sem"].at[m, 4 + half])

    def across_y(m):
        wait_ring(m)
        ysend[m][...] = total_of(m, 1 - y_hi).astype(BF16)
        send(ysend[m], yrecv[m], r["ys_sem"].at[m], r["yr_sem"].at[m], device(dy=2))
        own[m][y_hi] = total_of(m, y_hi)

    zs_sem, zr_sem = r["zs_sem"], r["zr_sem"]

    def owner_of(m, i):
        if WIDTH[m] == 256:
            return i, z
        return odd * 8 + i, lax.div(z, 2)

    def across_z(m):
        if EARLY[m]:
            wait_ring(m)
            total = jnp.concatenate([total_of(m, 0), total_of(m, 1)]).T
        else:
            wait(yrecv[m], r["yr_sem"].at[m])
            total = (own[m][y_hi] + yrecv[m][...].astype(F32)).T
        for i in range(WIDTH[m] // 16):
            for to in range(2):
                rows = total[16 * i + 8 * to : 16 * i + 8 * to + 8]
                zsend[m][i, to] = jnp.concatenate([rows[:, :128], rows[:, 128:]]).astype(BF16)

        def post(i, carry):
            to_z, slot = owner_of(m, i)

            def copy(to, sem):
                pltpu.make_async_remote_copy(
                    src_ref=zsend[m].at[i, to], dst_ref=zrecv[m].at[slot, core], send_sem=zs_sem.at[m, sem],
                    recv_sem=zr_sem.at[m, slot], device_id=device(dz=to_z - z, at=to), device_id_type=MESH,
                ).start()

            @pl.when(to_z != z)
            def _():
                copy(0, 0)
                copy(1, 0)

            @pl.when(to_z == z)
            def _():
                copy(other, 1)
                zrecv[m][slot, core] = zsend[m][i, core]

            return carry

        lax.fori_loop(0, WIDTH[m] // 16, post, 0)

    def owned(m):
        count = WIDTH[m] // 16

        def arrive(i, carry):
            from_z = i if count == NZ else 2 * i + lax.div(z, 8)

            @pl.when(from_z != z)
            def _():
                wait(zrecv[m].at[i], zr_sem.at[m, i])

            @pl.when(from_z == z)
            def _():
                wait(zrecv[m].at[i, other], zr_sem.at[m, i])

            return carry

        lax.fori_loop(0, count, arrive, 0)
        for half in range(2):
            total = zrecv[m][0, half].astype(F32)
            for i in range(1, count):
                total = total + zrecv[m][i, half].astype(F32)
            total = total * (1.0 / 256.0)
            for part in range(2):
                first = half * HK + part * 128
                wg_ref[m, :, first : first + 128] = total[8 * part : 8 * part + 8]

    def left(m):
        count = WIDTH[m] // 16
        to_self = (odd * 8 <= z) & (z < odd * 8 + 8)
        if count == NZ:
            wait(zsend[m].at[pl.ds(0, NZ - 1)], zs_sem.at[m, 0])
            wait(zsend[m].at[0, 0], zs_sem.at[m, 1])
            return

        @pl.when(to_self)
        def _():
            wait(zsend[m].at[pl.ds(0, count - 1)], zs_sem.at[m, 0])
            wait(zsend[m].at[0, 0], zs_sem.at[m, 1])

        @pl.when(jnp.logical_not(to_self))
        def _():
            wait(zsend[m], zs_sem.at[m, 0])

    def input_grad(b, carry):
        columns = aligned(b, Q)
        block, half = lax.div(b, 2), lax.rem(b, 2)
        rows = aligned(half, Q)
        total = lax.dot_general(gn[0], w[0, block, rows, :], NT, preferred_element_type=F32)
        total += lax.dot_general(gn[1], w[1, block, rows, :], NT, preferred_element_type=F32)

        @pl.when(core == 0)
        def _():
            igk[0, :, columns] = total[0:128]
            igk[1, :, columns] = total[256:384]
            igs[0, :, columns] = total[384:512].astype(BF16)
            igs[1, :, columns] = total[128:256].astype(BF16)

        @pl.when(core == 1)
        def _():
            igk[0, :, columns] = total[384:512]
            igk[1, :, columns] = total[128:256]
            igs[0, :, columns] = total[0:128].astype(BF16)
            igs[1, :, columns] = total[256:384].astype(BF16)

        return carry

    wait_partial(0)
    wait_partial(1)
    lax.fori_loop(0, 4, elementwise_hidden, 0)
    early = len(sent)
    order = (across, before, after, x)
    for block in order:
        pair(2, block)
    swap_y(2, across)
    wait_partial(2)
    lax.fori_loop(0, 4, elementwise_grads, 0)
    send_across(0)
    swap_y(2, before)
    send_near(0)
    for block in order:
        pair(1, block)
    swap_y(2, after)
    swap_y(2, x)
    lax.fori_loop(0, 4, input_grad, 0)
    send_across(2)
    swap_y(1, across)
    send_near(2)
    swap_y(1, before)
    send_far(0)
    keep(2)
    keep(0)
    swap_y(1, after)
    send_far(2)
    swap_y(1, x)
    send_across(1)
    lax.fori_loop(4, 8, input_grad, 0)
    send(igs, igr, r["is_sem"].at[0], r["ir_sem"].at[0], device(at=other))
    across_y(0)
    send_near(1)
    across_z(2)
    send_far(1)
    keep(1)
    drain(early)
    across_z(1)
    wait(igr, r["ir_sem"].at[0])
    for slot in (1, 0):
        igo[slot] = (igk[slot] + igr[slot].astype(F32)).astype(BF16)
    send(igo.at[1], ig_hbm.at[:, mine], r["is_sem"].at[1], r["ir_sem"].at[1], device(dy=-side))
    done = pltpu.make_async_copy(igo.at[0], ig_hbm.at[:, mine], local_sem.at[5])
    done.start()
    across_z(0)
    owned(2)
    left(2)
    owned(1)
    left(1)
    done.wait()
    wait(ig_hbm.at[:, theirs], r["ir_sem"].at[1])
    drain(len(sent))
    left(0)
    owned(0)


def local(tokens, grad_out, quant_weights, block_scales):
    any_space = pl.BlockSpec(memory_space=pl.ANY)
    vmem = pl.BlockSpec(memory_space=pltpu.VMEM)
    return pl.pallas_call(
        kernel,
        out_shape=(
            jax.ShapeDtypeStruct((TOK, 2 * HALF), BF16),
            jax.ShapeDtypeStruct((3, 8, 2 * HK), F32),
        ),
        in_specs=[any_space, any_space, any_space, vmem],
        out_specs=(any_space, vmem),
        scratch_shapes=list(scratch().values()),
        compiler_params=pltpu.CompilerParams(
            collective_id=0, has_side_effects=True, vmem_limit_bytes=56 * 1024 * 1024
        ),
    )(tokens, grad_out, quant_weights, block_scales)


def solution(mesh):
    return jax.shard_map(
        local,
        mesh=mesh,
        in_specs=(
            P(("inner", "outer"), None),
            P(("inner", "outer"), None),
            P(None, "inner", None, None),
            P(None, "inner", None),
        ),
        out_specs=(P(("inner", "outer"), None), P(None, ("inner", "outer"), None)),
        check_vma=False,
    )
```
